768 devices in a mesh: space: 192 (over x, z, y_hi, core), morder: 4 (over y_lo).
Axes of the slice: x: 4, y: 8 (y_hi: 2, y_lo: 4; y = y_hi * 4 + y_lo), z: 12, core: 2. Of those that a mesh axis runs over, the one named last changes fastest.
Arguments:
- nodes: bfloat16 [24576, 49, 128], P('space', None, 'morder'), may hold values from -6 to 6
- ghost_send: int32 [24576], P('space'), may hold values from 0 to 127, as said below
- edge_src: int32 [24576], P('space'), may hold values from 0 to 255
- edge_dst: int32 [24576], P('space'), may hold values from 0 to 127
- wigner: bfloat16 [24576, 29, 49], P('space'), may hold values from -6 to 6
- envelope: float32 [24576], P('space'), may hold values from 0.1 to 1
- w_zero: bfloat16 [896, 896], replicated, may hold values from -0.1875 to 0.1875
- w_one_real: bfloat16 [768, 768], replicated, may hold values from -0.15625 to 0.15625
- w_one_imag: bfloat16 [768, 768], replicated, may hold values from -0.15625 to 0.15625
- w_two_real: bfloat16 [640, 640], replicated, may hold values from -0.15625 to 0.15625
- w_two_imag: bfloat16 [640, 640], replicated, may hold values from -0.15625 to 0.15625
- cotangent: bfloat16 [24576, 49, 128], P('space', None, 'morder'), may hold values from -6 to 6
Outputs:
- updated: bfloat16 [24576, 49, 128], P('space', None, 'morder')
- node_grad: bfloat16 [24576, 49, 128], P('space', None, 'morder')
The draws below stay inside these ranges and needn't reach their ends.
Inputs may be any that keep to these rules, and one draw needn't show every extreme that they name: `ghost_send`: indices of atoms of the sending domain itself; the 128 entries of one domain are all different. `edge_src`: indices into the domain's extended list: own atoms, then lower ghosts, then upper ghosts. `edge_dst`: indices of the domain's own atoms.
All inputs are finite; a program needn't handle non-finite values.
Results may differ from the reference program's by a relative error of at most 0.0051.
Values may be sent and summed in bfloat16 or wider, within the bound.
A program may use at most 64 MiB of HBM per device.

```python
import jax
import jax.numpy as jnp
import numpy as np
from jax import lax

C = 128
K_NODE = 49
K_EDGE = 29
A_DEV = 128
GHOST = 64
E_DEV = 128
ATOMS = 24576
EDGES = 24576
N_SPACE = 192


def draw_ghost_send(key, part):
    key = jax.random.fold_in(key, 11)
    domain_keys = jax.random.split(key, N_SPACE)

    def one_domain(domain_key):
        return jax.random.permutation(domain_key, A_DEV)[:2 * GHOST]
    return jax.vmap(one_domain)(domain_keys).reshape(-1).astype(jnp.int32)


def place_ends(values, stream_key, low, largest):
    longest = values.shape.index(max(values.shape))
    spots = []
    for shift in (0, 1):
        where = [jax.random.randint(jax.random.fold_in(stream_key, axis), (), 0, length) for axis, length in enumerate(values.shape)]
        where[longest] = (where[longest] + shift) % values.shape[longest]
        spots.append(tuple(where))
    return values.at[spots[0]].set(low).at[spots[1]].set(largest)


def levels(rng, shape, pieces, smallest, top_value):
    loudness, own = 1.0, jax.random.fold_in(rng, 6)
    for position, parts in pieces:
        heights = jnp.exp(jax.random.uniform(jax.random.fold_in(own, position), (parts,), jnp.float32, smallest / len(pieces), top_value / len(pieces)))
        loudness = loudness * jnp.repeat(heights, shape[position] // parts).reshape([-1 if axis == position else 1 for axis in range(len(shape))])
    return loudness


def centred(rng, shape, deviation, limit, shards=(), kind=jnp.bfloat16):
    values = deviation * jax.random.normal(rng, shape, jnp.float32)
    if shards:
        values = values * levels(rng, shape, shards, -0.22, 0.18)
    return jnp.clip(values, -limit, limit).astype(kind)


def setup_inputs(seed: int = 0) -> dict:
    keys = jax.random.split(jax.random.key(seed), 13)
    return {
        "nodes": centred(keys[0], (ATOMS, K_NODE, C), 1.0, 6.0, ((0, 192), (2, 4))),
        "ghost_send": draw_ghost_send(jax.random.fold_in(keys[12], 71), 0),
        "edge_src": place_ends(jax.random.randint(keys[2], (EDGES,), 0, A_DEV + 2 * GHOST), jax.random.fold_in(keys[2], 1), 0, (A_DEV + 2 * GHOST) - 1).astype(jnp.int32),
        "edge_dst": place_ends(jax.random.randint(keys[3], (EDGES,), 0, A_DEV), jax.random.fold_in(keys[3], 1), 0, A_DEV - 1).astype(jnp.int32),
        "wigner": centred(keys[4], (EDGES, K_EDGE, K_NODE), 0.45, 6.0, ((0, 192),)),
        "envelope": jnp.clip(0.1 + 0.9 * jax.random.uniform(keys[5], (EDGES,), jnp.float32) ** levels(keys[5], (EDGES,), ((0, 192),), -0.2, 0.2), 0.1, 1.0),
        "w_zero": centred(keys[6], (7 * C, 7 * C), (7 * C) ** -0.5, 0.1875),
        "w_one_real": centred(keys[7], (6 * C, 6 * C), (12 * C) ** -0.5, 0.15625),
        "w_one_imag": centred(keys[8], (6 * C, 6 * C), (12 * C) ** -0.5, 0.15625),
        "w_two_real": centred(keys[9], (5 * C, 5 * C), (10 * C) ** -0.5, 0.15625),
        "w_two_imag": centred(keys[10], (5 * C, 5 * C), (10 * C) ** -0.5, 0.15625),
        "cotangent": centred(keys[11], (ATOMS, K_NODE, C), 1.0, 6.0, ((0, 192), (2, 4))),
    }


def block_mask():
    row_degree = list(range(7)) + list(range(1, 7)) * 2 + list(range(2, 7)) * 2
    column_degree = [degree for degree in range(7) for repeat in range(2 * degree + 1)]
    return (np.array(row_degree)[:, None] == np.array(column_degree)[None, :]).astype(np.float32)


def mix_block(coeffs, weight):
    return jnp.einsum("elc,lcmd->emd", coeffs.astype(jnp.float32), weight)


def mix_back(upstream, weight):
    return jnp.einsum("emd,lcmd->elc", upstream.astype(jnp.float32), weight)


def plane_forward(coeffs, weight_views):
    w_zero, w_one_real, w_one_imag, w_two_real, w_two_imag = weight_views
    first_plus, first_minus = coeffs[:, 7:13], coeffs[:, 13:19]
    second_plus, second_minus = coeffs[:, 19:24], coeffs[:, 24:29]
    return jnp.concatenate([
        mix_block(coeffs[:, 0:7], w_zero),
        mix_block(first_plus, w_one_real) - mix_block(first_minus, w_one_imag),
        mix_block(first_plus, w_one_imag) + mix_block(first_minus, w_one_real),
        mix_block(second_plus, w_two_real) - mix_block(second_minus, w_two_imag),
        mix_block(second_plus, w_two_imag) + mix_block(second_minus, w_two_real)], axis=1)


def plane_backward(upstream, weight_views):
    w_zero, w_one_real, w_one_imag, w_two_real, w_two_imag = weight_views
    first_plus, first_minus = upstream[:, 7:13], upstream[:, 13:19]
    second_plus, second_minus = upstream[:, 19:24], upstream[:, 24:29]
    return jnp.concatenate([
        mix_back(upstream[:, 0:7], w_zero),
        mix_back(first_plus, w_one_real) + mix_back(first_minus, w_one_imag),
        mix_back(first_minus, w_one_real) - mix_back(first_plus, w_one_imag),
        mix_back(second_plus, w_two_real) + mix_back(second_minus, w_two_imag),
        mix_back(second_minus, w_two_real) - mix_back(second_plus, w_two_imag)], axis=1)


def reference(nodes, ghost_send, edge_src, edge_dst, wigner, envelope, w_zero, w_one_real, w_one_imag, w_two_real, w_two_imag, cotangent):
    node_blocks = nodes.reshape(N_SPACE, A_DEV, K_NODE, C)
    cot_blocks = cotangent.reshape(N_SPACE, A_DEV, K_NODE, C)
    send_blocks = ghost_send.reshape(N_SPACE, 2 * GHOST)
    src_blocks = edge_src.reshape(N_SPACE, E_DEV)
    dst_blocks = edge_dst.reshape(N_SPACE, E_DEV)
    wig_blocks = wigner.reshape(N_SPACE, E_DEV, K_EDGE, K_NODE)
    env_blocks = envelope.reshape(N_SPACE, E_DEV)
    mask = jnp.asarray(block_mask(), jnp.float32)
    full_views = (w_zero.astype(jnp.float32).reshape(7, C, 7, C),
                  w_one_real.astype(jnp.float32).reshape(6, C, 6, C),
                  w_one_imag.astype(jnp.float32).reshape(6, C, 6, C),
                  w_two_real.astype(jnp.float32).reshape(5, C, 5, C),
                  w_two_imag.astype(jnp.float32).reshape(5, C, 5, C))

    def domain(index):
        before = (index + N_SPACE - 1) % N_SPACE
        after = (index + 1) % N_SPACE
        owned_rows = node_blocks[index]
        lower = node_blocks[before][send_blocks[before, GHOST:]]
        upper = node_blocks[after][send_blocks[after, :GHOST]]
        extended = jnp.concatenate([owned_rows, lower, upper], axis=0)
        rotation = wig_blocks[index].astype(jnp.float32) * mask
        edge_scale = env_blocks[index][:, None, None]
        source = extended[src_blocks[index]].astype(jnp.float32)
        rotated = jnp.einsum("ekn,enc->ekc", rotation, source).astype(jnp.bfloat16)
        message_rot = plane_forward(rotated, full_views).astype(jnp.bfloat16)
        message = edge_scale * jnp.einsum("ekn,ekc->enc", rotation, message_rot.astype(jnp.float32))
        aggregated = jnp.zeros((A_DEV, K_NODE, C), jnp.float32).at[dst_blocks[index]].add(message)
        updated = (owned_rows.astype(jnp.float32) + aggregated).astype(jnp.bfloat16)
        cot_rows = cot_blocks[index]
        upstream = cot_rows[dst_blocks[index]].astype(jnp.float32)
        edge_grad = (edge_scale * jnp.einsum("ekn,enc->ekc", rotation, upstream)).astype(jnp.bfloat16)
        rotated_grad = plane_backward(edge_grad, full_views).astype(jnp.bfloat16)
        source_grad = jnp.einsum("ekn,ekc->enc", rotation, rotated_grad.astype(jnp.float32))
        extended_grad = jnp.zeros((A_DEV + 2 * GHOST, K_NODE, C), jnp.float32).at[src_blocks[index]].add(source_grad)
        partial_grad = cot_rows.astype(jnp.float32) + extended_grad[:A_DEV]
        ghost_grad = extended_grad[A_DEV:].astype(jnp.bfloat16)
        return updated, partial_grad, ghost_grad

    updated, partial_grad, ghost_grad = lax.map(domain, jnp.arange(N_SPACE, dtype=jnp.int32))

    def finish(index):
        before = (index + N_SPACE - 1) % N_SPACE
        after = (index + 1) % N_SPACE
        total = partial_grad[index].at[send_blocks[index, :GHOST]].add(ghost_grad[before, GHOST:].astype(jnp.float32))
        total = total.at[send_blocks[index, GHOST:]].add(ghost_grad[after, :GHOST].astype(jnp.float32))
        return total.astype(jnp.bfloat16)

    node_grad = lax.map(finish, jnp.arange(N_SPACE, dtype=jnp.int32))
    return updated.reshape(ATOMS, K_NODE, C), node_grad.reshape(ATOMS, K_NODE, C)
```

```python
import functools

import jax
import jax.numpy as jnp
from jax import lax
from jax.experimental import pallas as pl
from jax.experimental.pallas import tpu as pltpu
from jax.sharding import PartitionSpec as P

F32, BF16 = jnp.float32, jnp.bfloat16
LANES = 128
TOP = 25
NODE = 49
EDGE = 29
WIDE = 1024
PARTS = ((0, 7), (7, 6), (13, 6), (19, 5), (24, 5))


def degree_rows(degree):
    rows = [degree]
    if degree >= 1:
        rows += [6 + degree, 12 + degree]
    if degree >= 2:
        rows += [17 + degree, 22 + degree]
    return rows


def dot(a, b):
    return jnp.dot(a, b, preferred_element_type=F32)


def dot_t(a, b):
    return lax.dot_general(a, b, (((1,), (1,)), ((), ())), preferred_element_type=F32)


def one_hot(index_row, offset=0):
    rows = lax.broadcasted_iota(jnp.int32, (LANES, LANES), 0) + offset
    return jnp.where(rows == index_row, 1.0, 0.0).astype(F32)


def lane_low():
    return lax.broadcasted_iota(jnp.int32, (LANES, LANES), 1) < LANES // 2


def row_low():
    return lax.broadcasted_iota(jnp.int32, (LANES, LANES), 0) < LANES // 2


def rotate(rot_ref, load, store):
    for degree in range(7):
        columns = range(degree * degree, (degree + 1) * (degree + 1))
        for k in degree_rows(degree):
            total = None
            for n in columns:
                term = rot_ref[n, k : k + 1, :].astype(F32) * load(n)
                total = term if total is None else total + term
            store(k, total)


def rotate_back(rot_ref, load, store):
    for degree in range(7):
        for n in range(degree * degree, (degree + 1) * (degree + 1)):
            total = None
            for k in degree_rows(degree):
                term = rot_ref[n, k : k + 1, :].astype(F32) * load(k)
                total = term if total is None else total + term
            store(n, total)


def channel_rows(n, count=1):
    return slice(n * 32, (n + count) * 32)


def swap_blocks(blocks):
    group = lax.broadcasted_iota(jnp.int32, blocks[0].shape, 1) // 32
    low = group < 2
    a0 = jnp.where(low, blocks[0], pltpu.roll(blocks[2], 64, 1))
    a2 = jnp.where(low, pltpu.roll(blocks[0], 64, 1), blocks[2])
    a1 = jnp.where(low, blocks[1], pltpu.roll(blocks[3], 64, 1))
    a3 = jnp.where(low, pltpu.roll(blocks[1], 64, 1), blocks[3])
    even = (group % 2) == 0
    b0 = jnp.where(even, a0, pltpu.roll(a1, 32, 1))
    b1 = jnp.where(even, pltpu.roll(a0, 96, 1), a1)
    b2 = jnp.where(even, a2, pltpu.roll(a3, 32, 1))
    b3 = jnp.where(even, pltpu.roll(a2, 96, 1), a3)
    return [b0, b1, b2, b3]


def store_transposed(rows_ref, out_ref):
    for block in range(WIDE // LANES):
        piece = rows_ref[block * LANES : (block + 1) * LANES, :].T.astype(BF16)
        for part in range(4):
            out_ref[part, :, block * LANES : (block + 1) * LANES] = piece[part * 32 : (part + 1) * 32]


def load_transposed(in_ref, rows_ref):
    for block in range(WIDE // LANES):
        piece = jnp.concatenate(
            [in_ref[part, :, block * LANES : (block + 1) * LANES].astype(F32) for part in range(4)],
            axis=0,
        )
        rows_ref[block * LANES : (block + 1) * LANES, :] = piece.T


def prepare(nodes, cot, wig, send, dst, env, low, high, edge_out, rows, hot):
    match = one_hot(send[...])
    turned = pltpu.roll(match, 64, 1)
    side = lane_low()
    zero = jnp.zeros((LANES, LANES), F32)
    first = jnp.concatenate([jnp.where(side, match, zero), jnp.where(side, zero, match)], 1).astype(BF16)
    second = jnp.concatenate([jnp.where(side, zero, turned), jnp.where(side, turned, zero)], 1).astype(BF16)
    for n in range(0, TOP, 5):
        both = dot(nodes[channel_rows(n, 5)], first)
        count = min(5, NODE - TOP - n)
        other = dot(nodes[channel_rows(TOP + n, count)], second)
        if count < 5:
            other = jnp.concatenate([other, jnp.zeros(((5 - count) * 32, 256), F32)], 0)
        both = (both + other).astype(BF16)
        low[channel_rows(n, 5)] = both[:, :LANES]
        high[channel_rows(n, 5)] = both[:, LANES:]
    hot[...] = dot(cot[...], one_hot(dst[...]).astype(BF16))
    scale = env[...]

    def store(k, value):
        rows[channel_rows(k)] = value * scale

    rotate(wig, lambda n: hot[channel_rows(n)], store)
    rows[EDGE * 32 :] = jnp.zeros((WIDE - EDGE * 32, LANES), F32)
    store_transposed(rows, edge_out)


def lower_rotate(nodes, below, above, wig, src, edge_out, rows, hot):
    side = row_low()
    index = src[...]
    zero = jnp.zeros((LANES, LANES), F32)
    own = one_hot(index).astype(BF16)
    plain = one_hot(index, LANES)
    up = one_hot(index, LANES + 64)
    down = one_hot(index, 64)
    above_top = jnp.where(side, up, zero).astype(BF16)
    below_top = jnp.where(side, zero, down).astype(BF16)
    below_bottom = jnp.where(side, plain, zero).astype(BF16)
    above_bottom = jnp.where(side, zero, plain).astype(BF16)
    split = TOP * 32
    rest = (NODE - TOP) * 32
    hot[:split] = dot(nodes[:split], own) + dot(below[...], below_top) + dot(above[...], above_top)
    hot[split:] = (
        dot(nodes[split:], own) + dot(below[:rest], below_bottom) + dot(above[:rest], above_bottom)
    )

    def store(k, value):
        rows[channel_rows(k)] = value

    rotate(wig, lambda n: hot[channel_rows(n)], store)
    rows[EDGE * 32 :] = jnp.zeros((WIDE - EDGE * 32, LANES), F32)
    store_transposed(rows, edge_out)


def gather_channels(in_ref):
    result = []
    for group in range(WIDE // LANES):
        blocks = [in_ref[i, :, group * LANES : (group + 1) * LANES].astype(F32) for i in range(4)]
        result += swap_blocks(blocks)
    return result[:EDGE]


def spread_channels(blocks, out_ref):
    blocks = blocks + [jnp.zeros_like(blocks[0])] * 3
    for group in range(WIDE // LANES):
        for i, value in enumerate(swap_blocks(blocks[4 * group : 4 * group + 4])):
            out_ref[i, :, group * LANES : (group + 1) * LANES] = value.astype(BF16)


def map_edges(forward, in_ref, w_zero, w_one_real, w_one_imag, w_two_real, w_two_imag, out_ref):
    blocks = gather_channels(in_ref)
    product = dot if forward else dot_t

    def part(i):
        start, count = PARTS[i]
        return jnp.concatenate(blocks[start : start + count], 1).astype(BF16)

    results = []

    def put(value):
        results.extend(value[:, i * LANES : (i + 1) * LANES] for i in range(value.shape[1] // LANES))

    put(product(part(0), w_zero[...]))
    for first, real, imag in ((1, w_one_real, w_one_imag), (3, w_two_real, w_two_imag)):
        both = jnp.concatenate([part(first), part(first + 1)], 0)
        straight = product(both, real[...])
        crossed = product(both, imag[...])
        if forward:
            put(straight[:32] - crossed[32:])
            put(straight[32:] + crossed[:32])
        else:
            put(straight[:32] + crossed[32:])
            put(straight[32:] - crossed[:32])
    spread_channels(results, out_ref)


def finish_forward(nodes, edge_in, wig, env, dst, updated, rows, hot):
    load_transposed(edge_in, rows)
    scale = env[...]

    def store(n, value):
        hot[channel_rows(n)] = (value * scale).astype(BF16)

    rotate_back(wig, lambda k: rows[channel_rows(k)], store)
    total = dot_t(hot[...], one_hot(dst[...]).astype(BF16))
    updated[...] = (nodes[...].astype(F32) + total).astype(BF16)


def scatter_back(edge_in, wig, src, own_grad, low, high, rows, hot):
    load_transposed(edge_in, rows)

    def store(n, value):
        hot[channel_rows(n)] = value.astype(BF16)

    rotate_back(wig, lambda k: rows[channel_rows(k)], store)
    index = src[...]
    side = row_low()
    zero = jnp.zeros((LANES, LANES), F32)
    plain = one_hot(index, LANES)
    up = one_hot(index, LANES + 64)
    down = one_hot(index, 64)
    first = jnp.concatenate([jnp.where(side, plain, zero), jnp.where(side, zero, plain)], 0).astype(BF16)
    second = jnp.concatenate([jnp.where(side, zero, down), jnp.where(side, up, zero)], 0).astype(BF16)
    for n in range(0, TOP, 5):
        both = dot_t(hot[channel_rows(n, 5)], first)
        count = min(5, NODE - TOP - n)
        other = dot_t(hot[channel_rows(TOP + n, count)], second)
        if count < 5:
            other = jnp.concatenate([other, jnp.zeros(((5 - count) * 32, 256), F32)], 0)
        both = (both + other).astype(BF16)
        low[channel_rows(n, 5)] = both[:, :LANES]
        high[channel_rows(n, 5)] = both[:, LANES:]
    own_grad[...] = dot_t(hot[...], one_hot(index).astype(BF16))


def finish_backward(cot, own_grad, below, above, send, node_grad):
    match = one_hot(send[...])
    turned = pltpu.roll(match, 64, 1)
    side = lane_low()
    zero = jnp.zeros((LANES, LANES), F32)
    split = TOP * 32
    rest = (NODE - TOP) * 32
    top = dot_t(above[...], jnp.where(side, turned, zero).astype(BF16)) + dot_t(
        below[...], jnp.where(side, zero, turned).astype(BF16)
    )
    bottom = dot_t(above[:rest], jnp.where(side, zero, match).astype(BF16)) + dot_t(
        below[:rest], jnp.where(side, match, zero).astype(BF16)
    )
    node_grad[:split] = (cot[:split].astype(F32) + own_grad[:split] + top).astype(BF16)
    node_grad[split:] = (cot[split:].astype(F32) + own_grad[split:] + bottom).astype(BF16)


def call(body, outs, scratch=()):
    return pl.pallas_call(
        body,
        out_shape=[jax.ShapeDtypeStruct(shape, dtype) for shape, dtype in outs],
        scratch_shapes=[pltpu.VMEM(shape, dtype) for shape, dtype in scratch],
        compiler_params=pltpu.CompilerParams(vmem_limit_bytes=40 * 1024 * 1024),
    )


def shards(
    nodes,
    ghost_send,
    edge_src,
    edge_dst,
    wigner,
    envelope,
    w_zero,
    w_one_real,
    w_one_imag,
    w_two_real,
    w_two_imag,
    cotangent,
):
    weights = (w_zero, w_one_real, w_one_imag, w_two_real, w_two_imag)
    flat = NODE * 32
    node_rows = jnp.transpose(nodes, (1, 2, 0)).reshape(flat, LANES)
    cot_rows = jnp.transpose(cotangent, (1, 2, 0)).reshape(flat, LANES)
    wig = jnp.transpose(wigner, (2, 1, 0))
    send = ghost_send.reshape(1, LANES)
    src = edge_src.reshape(1, LANES)
    dst = edge_dst.reshape(1, LANES)
    env = envelope.reshape(1, LANES)
    count = lax.axis_size("space")
    onward = [(i, (i + 1) % count) for i in range(count)]
    backward = [(target, source) for source, target in onward]
    ghost = ((TOP * 32, LANES), BF16)
    packed = ((4, 32, WIDE), BF16)
    rows = ((WIDE, LANES), F32)

    def exchange(x):
        return lax.all_to_all(x, "morder", split_axis=0, concat_axis=0, tiled=True)

    low, high, edge_grad = call(prepare, [ghost, ghost, packed], [rows, ((flat, LANES), F32)])(
        node_rows, cot_rows, wig, send, dst, env
    )
    below = lax.ppermute(high, "space", onward)
    above = lax.ppermute(low, "space", backward)
    edge_grad = exchange(edge_grad)
    (grad_back,) = call(functools.partial(map_edges, False), [packed])(edge_grad, *weights)
    grad_back = exchange(grad_back)
    own_grad, low_grad, high_grad = call(
        scatter_back, [((flat, LANES), F32), ghost, ghost], [rows, ((flat, LANES), BF16)]
    )(grad_back, wig, src)
    below_grad = lax.ppermute(high_grad, "space", onward)
    above_grad = lax.ppermute(low_grad, "space", backward)
    (rotated,) = call(lower_rotate, [packed], [rows, ((flat, LANES), F32)])(
        node_rows, below, above, wig, src
    )
    rotated = exchange(rotated)
    (message,) = call(functools.partial(map_edges, True), [packed])(rotated, *weights)
    message = exchange(message)
    (updated,) = call(finish_forward, [((flat, LANES), BF16)], [rows, ((flat, LANES), BF16)])(
        node_rows, message, wig, env, dst
    )
    (node_grad,) = call(finish_backward, [((flat, LANES), BF16)])(
        cot_rows, own_grad, below_grad, above_grad, send
    )

    def restore(x):
        return jnp.transpose(x.reshape(NODE, 32, LANES), (2, 0, 1))

    return restore(updated), restore(node_grad)


def solution(mesh):
    in_specs = (
        P("space", None, "morder"),
        P("space"),
        P("space"),
        P("space"),
        P("space", None, None),
        P("space"),
        P(),
        P(),
        P(),
        P(),
        P(),
        P("space", None, "morder"),
    )
    out_specs = (P("space", None, "morder"), P("space", None, "morder"))
    return jax.shard_map(shards, mesh=mesh, in_specs=in_specs, out_specs=out_specs, check_vma=False)
```

```python
import jax
import jax.numpy as jnp
from jax import lax
from jax.experimental import pallas as pl
from jax.experimental.pallas import tpu as pltpu
from jax.sharding import PartitionSpec as P

F32, BF16 = jnp.float32, jnp.bfloat16
LANES = 128
TOP = 25
NODE = 49
EDGE = 29
WIDE = 1024
PARTS = ((0, 7), (7, 6), (13, 6), (19, 5), (24, 5))


def degree_rows(degree):
    rows = [degree]
    if degree >= 1:
        rows += [6 + degree, 12 + degree]
    if degree >= 2:
        rows += [17 + degree, 22 + degree]
    return rows


def dot(a, b):
    return jnp.dot(a, b, preferred_element_type=F32)


def dot_t(a, b):
    return lax.dot_general(a, b, (((1,), (1,)), ((), ())), preferred_element_type=F32)


def one_hot(index_row, offset=0):
    rows = lax.broadcasted_iota(jnp.int32, (LANES, LANES), 0) + offset
    return jnp.where(rows == index_row, 1.0, 0.0).astype(F32)


def lane_low():
    return lax.broadcasted_iota(jnp.int32, (LANES, LANES), 1) < LANES // 2


def row_low():
    return lax.broadcasted_iota(jnp.int32, (LANES, LANES), 0) < LANES // 2


def rotate(rot_ref, load, store):
    for degree in range(7):
        columns = range(degree * degree, (degree + 1) * (degree + 1))
        for k in degree_rows(degree):
            total = None
            for n in columns:
                term = rot_ref[n, k : k + 1, :].astype(F32) * load(n)
                total = term if total is None else total + term
            store(k, total)


def rotate_back(rot_ref, load, store):
    for degree in range(7):
        for n in range(degree * degree, (degree + 1) * (degree + 1)):
            total = None
            for k in degree_rows(degree):
                term = rot_ref[n, k : k + 1, :].astype(F32) * load(k)
                total = term if total is None else total + term
            store(n, total)


def channel_rows(n, count=1):
    return slice(n * 32, (n + count) * 32)


def swap_blocks(blocks):
    group = lax.broadcasted_iota(jnp.int32, blocks[0].shape, 1) // 32
    low = group < 2
    a0 = jnp.where(low, blocks[0], pltpu.roll(blocks[2], 64, 1))
    a2 = jnp.where(low, pltpu.roll(blocks[0], 64, 1), blocks[2])
    a1 = jnp.where(low, blocks[1], pltpu.roll(blocks[3], 64, 1))
    a3 = jnp.where(low, pltpu.roll(blocks[1], 64, 1), blocks[3])
    even = (group % 2) == 0
    b0 = jnp.where(even, a0, pltpu.roll(a1, 32, 1))
    b1 = jnp.where(even, pltpu.roll(a0, 96, 1), a1)
    b2 = jnp.where(even, a2, pltpu.roll(a3, 32, 1))
    b3 = jnp.where(even, pltpu.roll(a2, 96, 1), a3)
    return [b0, b1, b2, b3]


CHUNKS = ((0, 2), (2, 5), (5, 8))


def store_transposed(rows_ref, out_ref, first, last):
    for group in range(first, last):
        piece = rows_ref[group * LANES : (group + 1) * LANES, :].T.astype(BF16)
        for part in range(4):
            out_ref[part, group] = piece[part * 32 : (part + 1) * 32]


def load_transposed(in_ref, rows_ref, first, last):
    for group in range(first, last):
        piece = jnp.concatenate([in_ref[part, group].astype(F32) for part in range(4)], axis=0)
        rows_ref[group * LANES : (group + 1) * LANES, :] = piece.T


class Exchange:
    def __init__(self, send, recv, send_sem, recv_sem, base):
        self.send, self.recv = send, recv
        self.space, self.me = lax.axis_index("space"), lax.axis_index("morder")
        self.copies = {}
        for piece, (first, last) in enumerate(CHUNKS):
            for step in (1, 2, 3):
                target = lax.rem(self.me + step, 4)
                slot = base + piece * 3 + step - 1
                span = pl.ds(first, last - first)
                self.copies[piece, step] = pltpu.make_async_remote_copy(
                    src_ref=send.at[target, span],
                    dst_ref=recv.at[self.me, span],
                    send_sem=send_sem.at[slot],
                    recv_sem=recv_sem.at[slot],
                    device_id=(self.space, target),
                    device_id_type=pl.DeviceIdType.MESH,
                )

    def start(self, piece):
        for step in (2, 1, 3):
            self.copies[piece, step].start()
        first, last = CHUNKS[piece]
        self.recv[self.me, first:last] = self.send[self.me, first:last]

    def arrived(self, piece):
        for step in (1, 2, 3):
            self.copies[piece, step].wait_recv()

    def sent(self):
        for copy in self.copies.values():
            copy.wait_send()


def gather_group(in_ref, group):
    return swap_blocks([in_ref[i, group].astype(F32) for i in range(4)])


def map_edges(forward, before, after, weights):
    w_zero, w_one_real, w_one_imag, w_two_real, w_two_imag = weights
    product = dot if forward else dot_t
    blocks, results = [], []

    def take(piece):
        before.arrived(piece)
        for group in range(*CHUNKS[piece]):
            blocks.extend(gather_group(before.recv, group))

    def part(i):
        start, count = PARTS[i]
        return jnp.concatenate(blocks[start : start + count], 1).astype(BF16)

    def put(value):
        results.extend(value[:, i * LANES : (i + 1) * LANES] for i in range(value.shape[1] // LANES))

    def pair(first, real, imag):
        both = jnp.concatenate([part(first), part(first + 1)], 0)
        straight = product(both, real[...])
        crossed = product(both, imag[...])
        if forward:
            put(straight[:32] - crossed[32:])
            put(straight[32:] + crossed[:32])
        else:
            put(straight[:32] + crossed[32:])
            put(straight[32:] - crossed[:32])

    def give(piece):
        for group in range(*CHUNKS[piece]):
            for i, value in enumerate(swap_blocks(results[4 * group : 4 * group + 4])):
                after.send[i, group] = value.astype(BF16)
        after.start(piece)

    take(0)
    put(product(part(0), w_zero[...]))
    take(1)
    pair(1, w_one_real, w_one_imag)
    give(0)
    take(2)
    pair(3, w_two_real, w_two_imag)
    give(1)
    results.extend([jnp.zeros_like(results[0])] * 3)
    give(2)


def ghost_pack(product, source, first, second, low, high):
    for n in range(0, TOP, 5):
        both = product(source[channel_rows(n, 5)], first)
        count = min(5, NODE - TOP - n)
        other = product(source[channel_rows(TOP + n, count)], second)
        if count < 5:
            other = jnp.concatenate([other, jnp.zeros(((5 - count) * 32, 256), F32)], 0)
        both = (both + other).astype(BF16)
        low[channel_rows(n, 5)] = both[:, :LANES]
        high[channel_rows(n, 5)] = both[:, LANES:]


def layer(
    nodes_hbm,
    cot_hbm,
    wig_hbm,
    send_ref,
    src_ref,
    dst_ref,
    env_ref,
    w0_hbm,
    w1r_hbm,
    w1i_hbm,
    w2r_hbm,
    w2i_hbm,
    updated_hbm,
    node_grad_hbm,
    nodes,
    cot,
    wig,
    w0,
    w1r,
    w1i,
    w2r,
    w2i,
    low,
    high,
    below,
    above,
    low_grad,
    high_grad,
    below_grad,
    above_grad,
    edge_send,
    edge_recv,
    back_send,
    back_recv,
    rot_send,
    rot_recv,
    msg_send,
    msg_recv,
    rows,
    hot,
    hot_half,
    own_grad,
    updated,
    node_grad,
    local_sem,
    out_sem,
    send_sem,
    recv_sem,
    ghost_send_sem,
    ghost_recv_sem,
):
    space, me = lax.axis_index("space"), lax.axis_index("morder")
    domains = lax.axis_size("space")
    upper = lax.rem(space + 1, domains)
    lower = lax.rem(space + domains - 1, domains)
    peers = [(upper, me), (lower, me)] + [(space, lax.rem(me + step, 4)) for step in (1, 2, 3)]
    barrier = pltpu.get_barrier_semaphore()
    for peer in peers:
        pl.semaphore_signal(barrier, inc=1, device_id=peer, device_id_type=pl.DeviceIdType.MESH)
    loads = [
        pltpu.make_async_copy(a, b, local_sem.at[i])
        for i, (a, b) in enumerate(
            (
                (cot_hbm, cot),
                (wig_hbm, wig),
                (nodes_hbm, nodes),
                (w0_hbm, w0),
                (w1r_hbm, w1r),
                (w1i_hbm, w1i),
                (w2r_hbm, w2r),
                (w2i_hbm, w2i),
            )
        )
    ]
    for load in loads:
        load.start()
    weights = (w0, w1r, w1i, w2r, w2i)

    def ghost_copy(slot, source, target, device):
        return pltpu.make_async_remote_copy(
            src_ref=source,
            dst_ref=target,
            send_sem=ghost_send_sem.at[slot],
            recv_sem=ghost_recv_sem.at[slot],
            device_id=(device, me),
            device_id_type=pl.DeviceIdType.MESH,
        )

    ghosts = [
        ghost_copy(0, high, below, upper),
        ghost_copy(1, low, above, lower),
        ghost_copy(2, high_grad, below_grad, upper),
        ghost_copy(3, low_grad, above_grad, lower),
    ]
    pieces = len(CHUNKS) * 3
    edge_x = Exchange(edge_send, edge_recv, send_sem, recv_sem, 0)
    back_x = Exchange(back_send, back_recv, send_sem, recv_sem, pieces)
    rot_x = Exchange(rot_send, rot_recv, send_sem, recv_sem, 2 * pieces)
    msg_x = Exchange(msg_send, msg_recv, send_sem, recv_sem, 3 * pieces)

    side, rside = lane_low(), row_low()
    zero = jnp.zeros((LANES, LANES), F32)
    scale = env_ref[...]
    rows[EDGE * 32 :] = jnp.zeros((WIDE - EDGE * 32, LANES), F32)
    split = TOP * 32
    rest = (NODE - TOP) * 32

    loads[0].wait()
    hot[...] = dot(cot[...], one_hot(dst_ref[...]).astype(BF16))
    loads[1].wait()

    def store_scaled(k, value):
        rows[channel_rows(k)] = value * scale

    def store_plain(k, value):
        rows[channel_rows(k)] = value

    rotate(wig, lambda n: hot[channel_rows(n)], store_scaled)
    for piece, (first, last) in enumerate(CHUNKS):
        store_transposed(rows, edge_send, first, last)
        if piece == 0:
            pl.semaphore_wait(barrier, len(peers))
        edge_x.start(piece)

    match = one_hot(send_ref[...])
    turned = pltpu.roll(match, 64, 1)
    loads[2].wait()
    ghost_pack(
        dot,
        nodes,
        jnp.concatenate([jnp.where(side, match, zero), jnp.where(side, zero, match)], 1).astype(BF16),
        jnp.concatenate([jnp.where(side, zero, turned), jnp.where(side, turned, zero)], 1).astype(BF16),
        low,
        high,
    )
    ghosts[0].start()
    ghosts[1].start()
    index = src_ref[...]
    own = one_hot(index).astype(BF16)
    plain = one_hot(index, LANES)
    up = one_hot(index, LANES + 64)
    down = one_hot(index, 64)
    hot[...] = dot(nodes[...], own)

    for load in loads[3:]:
        load.wait()
    map_edges(False, edge_x, back_x, weights)

    ghosts[0].wait_recv()
    ghosts[1].wait_recv()
    hot[:split] += dot(below[...], jnp.where(rside, zero, down).astype(BF16)) + dot(
        above[...], jnp.where(rside, up, zero).astype(BF16)
    )
    hot[split:] += dot(below[:rest], jnp.where(rside, plain, zero).astype(BF16)) + dot(
        above[:rest], jnp.where(rside, zero, plain).astype(BF16)
    )
    rotate(wig, lambda n: hot[channel_rows(n)], store_plain)
    for piece, (first, last) in enumerate(CHUNKS):
        store_transposed(rows, rot_send, first, last)
        rot_x.start(piece)

    for piece, (first, last) in enumerate(CHUNKS):
        back_x.arrived(piece)
        load_transposed(back_recv, rows, first, last)

    def store_half(n, value):
        hot_half[channel_rows(n)] = value.astype(BF16)

    rotate_back(wig, lambda k: rows[channel_rows(k)], store_half)
    ghost_pack(
        dot_t,
        hot_half,
        jnp.concatenate([jnp.where(rside, plain, zero), jnp.where(rside, zero, plain)], 0).astype(BF16),
        jnp.concatenate([jnp.where(rside, zero, down), jnp.where(rside, up, zero)], 0).astype(BF16),
        low_grad,
        high_grad,
    )
    ghosts[2].start()
    ghosts[3].start()
    own_grad[...] = dot_t(hot_half[...], own) + cot[...].astype(F32)

    map_edges(True, rot_x, msg_x, weights)

    for piece, (first, last) in enumerate(CHUNKS):
        msg_x.arrived(piece)
        load_transposed(msg_recv, rows, first, last)

    def store_message(n, value):
        hot_half[channel_rows(n)] = (value * scale).astype(BF16)

    rotate_back(wig, lambda k: rows[channel_rows(k)], store_message)
    total = dot_t(hot_half[...], one_hot(dst_ref[...]).astype(BF16))
    updated[...] = (nodes[...].astype(F32) + total).astype(BF16)
    write = pltpu.make_async_copy(updated, updated_hbm, out_sem.at[0])
    write.start()

    ghosts[2].wait_recv()
    ghosts[3].wait_recv()
    match = one_hot(send_ref[...])
    turned = pltpu.roll(match, 64, 1)
    top = dot_t(above_grad[...], jnp.where(side, turned, zero).astype(BF16)) + dot_t(
        below_grad[...], jnp.where(side, zero, turned).astype(BF16)
    )
    node_grad[:split] = (own_grad[:split] + top).astype(BF16)
    bottom = dot_t(above_grad[:rest], jnp.where(side, zero, match).astype(BF16)) + dot_t(
        below_grad[:rest], jnp.where(side, match, zero).astype(BF16)
    )
    node_grad[split:] = (own_grad[split:] + bottom).astype(BF16)
    last_write = pltpu.make_async_copy(node_grad, node_grad_hbm, out_sem.at[1])
    last_write.start()
    for x in (edge_x, back_x, rot_x, msg_x):
        x.sent()
    for copy in ghosts:
        copy.wait_send()
    write.wait()
    last_write.wait()


def shards(
    nodes,
    ghost_send,
    edge_src,
    edge_dst,
    wigner,
    envelope,
    w_zero,
    w_one_real,
    w_one_imag,
    w_two_real,
    w_two_imag,
    cotangent,
):
    flat = NODE * 32
    node_rows = jnp.transpose(nodes, (1, 2, 0)).reshape(flat, LANES)
    cot_rows = jnp.transpose(cotangent, (1, 2, 0)).reshape(flat, LANES)
    wig = jnp.transpose(wigner, (2, 1, 0))
    atoms = pltpu.VMEM((flat, LANES), BF16)
    ghost = pltpu.VMEM((TOP * 32, LANES), BF16)
    packed = pltpu.VMEM((4, WIDE // LANES, 32, LANES), BF16)
    weights = (w_zero, w_one_real, w_one_imag, w_two_real, w_two_imag)
    copies = 4 * 3 * len(CHUNKS)
    anywhere = pl.BlockSpec(memory_space=pltpu.HBM)
    vmem = pl.BlockSpec(memory_space=pltpu.VMEM)
    updated, node_grad = pl.pallas_call(
        layer,
        out_shape=[jax.ShapeDtypeStruct((flat, LANES), BF16)] * 2,
        in_specs=[anywhere] * 3 + [vmem] * 4 + [anywhere] * 5,
        out_specs=[anywhere] * 2,
        scratch_shapes=[atoms, atoms, pltpu.VMEM(wig.shape, BF16)]
        + [pltpu.VMEM(w.shape, BF16) for w in weights]
        + [ghost] * 8
        + [packed] * 8
        + [
            pltpu.VMEM((WIDE, LANES), F32),
            pltpu.VMEM((flat, LANES), F32),
            atoms,
            pltpu.VMEM((flat, LANES), F32),
            atoms,
            atoms,
            pltpu.SemaphoreType.DMA((8,)),
            pltpu.SemaphoreType.DMA((2,)),
            pltpu.SemaphoreType.DMA((copies,)),
            pltpu.SemaphoreType.DMA((copies,)),
            pltpu.SemaphoreType.DMA((4,)),
            pltpu.SemaphoreType.DMA((4,)),
        ],
        compiler_params=pltpu.CompilerParams(
            vmem_limit_bytes=60 * 1024 * 1024, collective_id=0, has_side_effects=True
        ),
    )(
        node_rows,
        cot_rows,
        wig,
        ghost_send.reshape(1, LANES),
        edge_src.reshape(1, LANES),
        edge_dst.reshape(1, LANES),
        envelope.reshape(1, LANES),
        *weights,
    )

    def restore(x):
        return jnp.transpose(x.reshape(NODE, 32, LANES), (2, 0, 1))

    return restore(updated), restore(node_grad)


def solution(mesh):
    in_specs = (
        P("space", None, "morder"),
        P("space"),
        P("space"),
        P("space"),
        P("space", None, None),
        P("space"),
        P(),
        P(),
        P(),
        P(),
        P(),
        P("space", None, "morder"),
    )
    out_specs = (P("space", None, "morder"), P("space", None, "morder"))
    return jax.shard_map(shards, mesh=mesh, in_specs=in_specs, out_specs=out_specs, check_vma=False)
```

```python
import jax
import jax.numpy as jnp
from jax import lax
from jax.experimental import pallas as pl
from jax.experimental.pallas import tpu as pltpu
from jax.sharding import PartitionSpec as P

F32, BF16 = jnp.float32, jnp.bfloat16
LANES = 128
HALF = 784
NODE = 49
EDGE = 29
PACKED = 240
PARTS = ((0, 6), (6, 6), (12, 5), (17, 5), (22, 7))


def degree_rows(degree):
    rows = [degree]
    if degree >= 1:
        rows += [6 + degree, 12 + degree]
    if degree >= 2:
        rows += [17 + degree, 22 + degree]
    return rows


def dot(a, b):
    return jnp.dot(a, b, preferred_element_type=F32)


def dot_t(a, b):
    return lax.dot_general(a, b, (((1,), (1,)), ((), ())), preferred_element_type=F32)


def one_hot(index_row, offset=0):
    rows = lax.broadcasted_iota(jnp.int32, (LANES, LANES), 0) + offset
    return jnp.where(rows == index_row, 1.0, 0.0).astype(F32)


def lane_low():
    return lax.broadcasted_iota(jnp.int32, (LANES, LANES), 1) < LANES // 2


def row_low():
    return lax.broadcasted_iota(jnp.int32, (LANES, LANES), 0) < LANES // 2


def rotate(rot_ref, load, store):
    for degree in range(7):
        columns = range(degree * degree, (degree + 1) * (degree + 1))
        for k in degree_rows(degree):
            total = None
            for n in columns:
                term = rot_ref[n, k : k + 1, :].astype(F32) * load(n)
                total = term if total is None else total + term
            store(k, total)


def rotate_back(rot_ref, load, store):
    for degree in range(7):
        for n in range(degree * degree, (degree + 1) * (degree + 1)):
            total = None
            for k in degree_rows(degree):
                term = rot_ref[n, k : k + 1, :].astype(F32) * load(k)
                total = term if total is None else total + term
            store(n, total)


def place(k):
    return k - 7 if k >= 7 else k + 22


def channel_rows(n, count=1):
    return slice(n * 32, (n + count) * 32)


def swap_blocks(blocks):
    group = lax.broadcasted_iota(jnp.int32, blocks[0].shape, 1) // 32
    low = group < 2
    a0 = jnp.where(low, blocks[0], pltpu.roll(blocks[2], 64, 1))
    a2 = jnp.where(low, pltpu.roll(blocks[0], 64, 1), blocks[2])
    a1 = jnp.where(low, blocks[1], pltpu.roll(blocks[3], 64, 1))
    a3 = jnp.where(low, pltpu.roll(blocks[1], 64, 1), blocks[3])
    even = (group % 2) == 0
    b0 = jnp.where(even, a0, pltpu.roll(a1, 32, 1))
    b1 = jnp.where(even, pltpu.roll(a0, 96, 1), a1)
    b2 = jnp.where(even, a2, pltpu.roll(a3, 32, 1))
    b3 = jnp.where(even, pltpu.roll(a2, 96, 1), a3)
    return [b0, b1, b2, b3]


CHUNKS = ((0, 3), (3, 8))


def span_of(group):
    return slice(group * 32, min(group * 32 + 32, PACKED))


def fold(block):
    lane = lax.broadcasted_iota(jnp.int32, (16, LANES), 1)
    return jnp.where(lane < 32, block[:16], pltpu.roll(block[16:], 32, 1))


def unfold(block):
    return jnp.concatenate([block, pltpu.roll(block, 96, 1)], 0)


def store_transposed(rows_ref, out_ref, first, last):
    for group in range(first, last):
        piece = rows_ref[group * LANES : (group + 1) * LANES, :].T
        for part in range(4):
            block = piece[part * 32 : (part + 1) * 32]
            if group == 7:
                block = fold(block)
            out_ref[part, span_of(group)] = block.astype(BF16)


def load_group(in_ref, part, group):
    block = in_ref[part, span_of(group)].astype(F32)
    return unfold(block) if group == 7 else block


def load_transposed(in_ref, rows_ref, first, last):
    for group in range(first, last):
        piece = jnp.concatenate([load_group(in_ref, part, group) for part in range(4)], axis=0)
        rows_ref[group * LANES : (group + 1) * LANES, :] = piece.T


def piece_span(piece):
    first, last = CHUNKS[piece]
    return pl.ds(first * 32, min(last * 32, PACKED) - first * 32)


class Exchange:
    def __init__(self, send, recv, send_sem, recv_sem, base, kept_sem=None):
        self.send, self.recv = send, recv
        self.space, self.me = lax.axis_index("space"), lax.axis_index("morder")
        self.copies = {}
        self.kept = []
        for piece in range(len(CHUNKS)):
            if kept_sem is not None:
                span = piece_span(piece)
                self.kept.append(
                    pltpu.make_async_copy(send.at[self.me, span], recv.at[self.me, span], kept_sem.at[piece])
                )
            for step in (1, 2, 3):
                target = lax.rem(self.me + step, 4)
                slot = base + piece * 3 + step - 1
                span = piece_span(piece)
                self.copies[piece, step] = pltpu.make_async_remote_copy(
                    src_ref=send.at[target, span],
                    dst_ref=recv.at[self.me, span],
                    send_sem=send_sem.at[slot],
                    recv_sem=recv_sem.at[slot],
                    device_id=(self.space, target),
                    device_id_type=pl.DeviceIdType.MESH,
                )

    def start(self, piece):
        for step in (2, 1, 3):
            self.copies[piece, step].start()
        if self.kept:
            self.kept[piece].start()
        else:
            span = piece_span(piece)
            self.recv[self.me, span] = self.send[self.me, span]

    def arrived(self, piece):
        for step in (1, 2, 3):
            self.copies[piece, step].wait_recv()

    def sent(self):
        for copy in self.kept:
            copy.wait()
        for copy in self.copies.values():
            copy.wait_send()


def gather_group(in_ref, group):
    return swap_blocks([load_group(in_ref, i, group) for i in range(4)])


def map_edges(forward, before, after, weights):
    w_zero, w_one_real, w_one_imag, w_two_real, w_two_imag = weights
    product = dot if forward else dot_t
    blocks, results = [], []

    def take(piece):
        before.arrived(piece)
        for group in range(*CHUNKS[piece]):
            blocks.extend(gather_group(before.recv, group))

    def part(i):
        start, count = PARTS[i]
        return jnp.concatenate(blocks[start : start + count], 1).astype(BF16)

    def put(value):
        results.extend(value[:, i * LANES : (i + 1) * LANES] for i in range(value.shape[1] // LANES))

    def pair(first, real, imag):
        both = jnp.concatenate([part(first), part(first + 1)], 0)
        straight = product(both, real[...])
        crossed = product(both, imag[...])
        if forward:
            put(straight[:32] - crossed[32:])
            put(straight[32:] + crossed[:32])
        else:
            put(straight[:32] + crossed[32:])
            put(straight[32:] - crossed[:32])

    def give(piece):
        for group in range(*CHUNKS[piece]):
            for i, value in enumerate(swap_blocks(results[4 * group : 4 * group + 4])):
                if group == 7:
                    value = fold(value)
                after.send[i, span_of(group)] = value.astype(BF16)
        after.start(piece)

    take(0)
    pair(0, w_one_real, w_one_imag)
    give(0)
    take(1)
    pair(2, w_two_real, w_two_imag)
    put(product(part(4), w_zero[...]))
    results.extend([jnp.zeros_like(results[0])] * 3)
    give(1)


def ghost_pack(product, source, first, second, low, high):
    for row in range(0, HALF, 112):
        both = product(source[row : row + 112], first) + product(source[HALF + row : HALF + row + 112], second)
        both = both.astype(BF16)
        low[row : row + 112] = both[:, :LANES]
        high[row : row + 112] = both[:, LANES:]


def layer(
    nodes_hbm,
    cot_hbm,
    wig_hbm,
    send_ref,
    src_ref,
    dst_ref,
    env_ref,
    w0_hbm,
    w1r_hbm,
    w1i_hbm,
    w2r_hbm,
    w2i_hbm,
    msg_recv,
    own_hbm,
    below_grad,
    above_grad,
    nodes,
    cot,
    wig,
    w0,
    w1r,
    w1i,
    w2r,
    w2i,
    low,
    high,
    below,
    above,
    low_grad,
    high_grad,
    edge_send,
    edge_recv,
    back_send,
    back_recv,
    rot_send,
    rot_recv,
    msg_send,
    rows,
    hot,
    hot_half,
    own_grad,
    local_sem,
    out_sem,
    kept_sem,
    send_sem,
    recv_sem,
    ghost_send_sem,
    ghost_recv_sem,
):
    space, me = lax.axis_index("space"), lax.axis_index("morder")
    domains = lax.axis_size("space")
    upper = lax.rem(space + 1, domains)
    lower = lax.rem(space + domains - 1, domains)
    peers = [(upper, me), (lower, me)] + [(space, lax.rem(me + step, 4)) for step in (1, 2, 3)]
    barrier = pltpu.get_barrier_semaphore()
    for peer in peers:
        pl.semaphore_signal(barrier, inc=1, device_id=peer, device_id_type=pl.DeviceIdType.MESH)
    loads = [
        pltpu.make_async_copy(a, b, local_sem.at[i])
        for i, (a, b) in enumerate(
            (
                (cot_hbm, cot),
                (wig_hbm, wig),
                (nodes_hbm, nodes),
                (w0_hbm, w0),
                (w1r_hbm, w1r),
                (w1i_hbm, w1i),
                (w2r_hbm, w2r),
                (w2i_hbm, w2i),
            )
        )
    ]
    for load in loads:
        load.start()
    weights = (w0, w1r, w1i, w2r, w2i)

    def ghost_copy(slot, source, target, device):
        return pltpu.make_async_remote_copy(
            src_ref=source,
            dst_ref=target,
            send_sem=ghost_send_sem.at[slot],
            recv_sem=ghost_recv_sem.at[slot],
            device_id=(device, me),
            device_id_type=pl.DeviceIdType.MESH,
        )

    ghosts = [
        ghost_copy(0, high, below, upper),
        ghost_copy(1, low, above, lower),
        ghost_copy(2, high_grad, below_grad, upper),
        ghost_copy(3, low_grad, above_grad, lower),
    ]
    pieces = len(CHUNKS) * 3
    edge_x = Exchange(edge_send, edge_recv, send_sem, recv_sem, 0)
    back_x = Exchange(back_send, back_recv, send_sem, recv_sem, pieces)
    rot_x = Exchange(rot_send, rot_recv, send_sem, recv_sem, 2 * pieces)
    msg_x = Exchange(msg_send, msg_recv, send_sem, recv_sem, 3 * pieces, kept_sem)

    side, rside = lane_low(), row_low()
    zero = jnp.zeros((LANES, LANES), F32)
    scale = env_ref[...]
    rows[EDGE * 32 :] = jnp.zeros((8 * LANES - EDGE * 32, LANES), F32)

    loads[0].wait()
    hot[...] = dot(cot[...], one_hot(dst_ref[...]).astype(BF16))
    loads[1].wait()

    def store_scaled(k, value):
        rows[channel_rows(place(k))] = value * scale

    def store_plain(k, value):
        rows[channel_rows(place(k))] = value

    rotate(wig, lambda n: hot[channel_rows(n)], store_scaled)
    for piece, (first, last) in enumerate(CHUNKS):
        store_transposed(rows, edge_send, first, last)
        if piece == 0:
            pl.semaphore_wait(barrier, len(peers))
        edge_x.start(piece)

    edge_x.sent()
    match = one_hot(send_ref[...])
    turned = pltpu.roll(match, 64, 1)
    loads[2].wait()
    ghost_pack(
        dot,
        nodes,
        jnp.concatenate([jnp.where(side, match, zero), jnp.where(side, zero, match)], 1).astype(BF16),
        jnp.concatenate([jnp.where(side, zero, turned), jnp.where(side, turned, zero)], 1).astype(BF16),
        low,
        high,
    )
    ghosts[0].start()
    ghosts[1].start()
    index = src_ref[...]
    own = one_hot(index).astype(BF16)
    plain = one_hot(index, LANES)
    up = one_hot(index, LANES + 64)
    down = one_hot(index, 64)
    hot[...] = dot(nodes[...], own)

    for load in loads[3:]:
        load.wait()
    map_edges(False, edge_x, back_x, weights)

    ghosts[0].wait_recv()
    ghosts[1].wait_recv()
    hot[:HALF] += dot(below[...], jnp.where(rside, zero, down).astype(BF16)) + dot(
        above[...], jnp.where(rside, up, zero).astype(BF16)
    )
    hot[HALF:] += dot(below[...], jnp.where(rside, plain, zero).astype(BF16)) + dot(
        above[...], jnp.where(rside, zero, plain).astype(BF16)
    )
    rotate(wig, lambda n: hot[channel_rows(n)], store_plain)
    for piece, (first, last) in enumerate(CHUNKS):
        store_transposed(rows, rot_send, first, last)
        rot_x.start(piece)

    for piece, (first, last) in enumerate(CHUNKS):
        back_x.arrived(piece)
        load_transposed(back_recv, rows, first, last)

    def store_half(n, value):
        hot_half[channel_rows(n)] = value.astype(BF16)

    rotate_back(wig, lambda k: rows[channel_rows(place(k))], store_half)
    ghost_pack(
        dot_t,
        hot_half,
        jnp.concatenate([jnp.where(rside, plain, zero), jnp.where(rside, zero, plain)], 0).astype(BF16),
        jnp.concatenate([jnp.where(rside, zero, down), jnp.where(rside, up, zero)], 0).astype(BF16),
        low_grad,
        high_grad,
    )
    ghosts[2].start()
    ghosts[3].start()
    own_grad[...] = dot_t(hot_half[...], own) + cot[...].astype(F32)
    last_write = pltpu.make_async_copy(own_grad, own_hbm, out_sem.at[0])
    last_write.start()

    map_edges(True, rot_x, msg_x, weights)

    for piece in range(len(CHUNKS)):
        msg_x.arrived(piece)
    ghosts[2].wait_recv()
    ghosts[3].wait_recv()
    for x in (back_x, rot_x, msg_x):
        x.sent()
    for copy in ghosts:
        copy.wait_send()
    last_write.wait()


def finish(
    msg_hbm,
    wig_hbm,
    nodes_hbm,
    own_hbm,
    below_hbm,
    above_hbm,
    send_ref,
    dst_ref,
    env_ref,
    updated_hbm,
    grad_hbm,
    msg,
    wig,
    nodes,
    own,
    below,
    above,
    rows,
    hot,
    updated,
    grad,
    sem,
    out_sem,
):
    loads = [
        pltpu.make_async_copy(a, b, sem.at[i])
        for i, (a, b) in enumerate(
            (
                (msg_hbm, msg),
                (wig_hbm, wig),
                (nodes_hbm, nodes),
                (above_hbm, above),
                (below_hbm, below),
                (own_hbm, own),
            )
        )
    ]
    for load in loads:
        load.start()
    match = one_hot(send_ref[...])
    turned = pltpu.roll(match, 64, 1)
    side = lane_low()
    zero = jnp.zeros((LANES, LANES), F32)
    pairs = (
        (jnp.where(side, turned, zero), jnp.where(side, zero, turned)),
        (jnp.where(side, zero, match), jnp.where(side, match, zero)),
    )
    target = one_hot(dst_ref[...]).astype(BF16)
    scale = env_ref[...]
    loads[0].wait()
    load_transposed(msg, rows, 0, 8)
    loads[1].wait()

    def store_message(n, value):
        hot[channel_rows(n)] = (value * scale).astype(BF16)

    rotate_back(wig, lambda k: rows[channel_rows(place(k))], store_message)
    loads[2].wait()
    updated[...] = (nodes[...].astype(F32) + dot_t(hot[...], target)).astype(BF16)
    writes = [pltpu.make_async_copy(updated, updated_hbm, out_sem.at[0])]
    writes[0].start()
    for load in loads[3:]:
        load.wait()
    for half, (for_above, for_below) in enumerate(pairs):
        span = pl.ds(half * HALF, HALF)
        total = dot_t(above[...], for_above.astype(BF16)) + dot_t(below[...], for_below.astype(BF16))
        grad[span] = (own[span] + total).astype(BF16)
        writes.append(pltpu.make_async_copy(grad.at[span], grad_hbm.at[span], out_sem.at[1 + half]))
        writes[-1].start()
    for write in writes:
        write.wait()


def shards(
    nodes,
    ghost_send,
    edge_src,
    edge_dst,
    wigner,
    envelope,
    w_zero,
    w_one_real,
    w_one_imag,
    w_two_real,
    w_two_imag,
    cotangent,
):
    flat = NODE * 32
    node_rows = jnp.transpose(nodes, (1, 2, 0)).reshape(flat, LANES)
    cot_rows = jnp.transpose(cotangent, (1, 2, 0)).reshape(flat, LANES)
    wig = jnp.transpose(wigner, (2, 1, 0))
    atoms = pltpu.VMEM((flat, LANES), BF16)
    ghost = pltpu.VMEM((HALF, LANES), BF16)
    packed = pltpu.VMEM((4, PACKED, LANES), BF16)
    weights = (w_zero, w_one_real, w_one_imag, w_two_real, w_two_imag)
    copies = 4 * 3 * len(CHUNKS)
    anywhere = pl.BlockSpec(memory_space=pltpu.HBM)
    vmem = pl.BlockSpec(memory_space=pltpu.VMEM)
    rows16 = jax.ShapeDtypeStruct((flat, LANES), BF16)
    rows32 = jax.ShapeDtypeStruct((flat, LANES), F32)
    returned = jax.ShapeDtypeStruct((HALF, LANES), BF16)
    send = ghost_send.reshape(1, LANES)
    dst = edge_dst.reshape(1, LANES)
    env = envelope.reshape(1, LANES)
    message, own_grad, below_grad, above_grad = pl.pallas_call(
        layer,
        out_shape=[jax.ShapeDtypeStruct((4, PACKED, LANES), BF16), rows32, returned, returned],
        in_specs=[anywhere] * 3 + [vmem] * 4 + [anywhere] * 5,
        out_specs=[anywhere] * 4,
        scratch_shapes=[atoms, atoms, pltpu.VMEM(wig.shape, BF16)]
        + [pltpu.VMEM(w.shape, BF16) for w in weights]
        + [ghost] * 6
        + [packed] * 7
        + [
            pltpu.VMEM((8 * LANES, LANES), F32),
            pltpu.VMEM((flat, LANES), F32),
            atoms,
            pltpu.VMEM((flat, LANES), F32),
            pltpu.SemaphoreType.DMA((8,)),
            pltpu.SemaphoreType.DMA((1,)),
            pltpu.SemaphoreType.DMA((len(CHUNKS),)),
            pltpu.SemaphoreType.DMA((copies,)),
            pltpu.SemaphoreType.DMA((copies,)),
            pltpu.SemaphoreType.DMA((4,)),
            pltpu.SemaphoreType.DMA((4,)),
        ],
        compiler_params=pltpu.CompilerParams(
            vmem_limit_bytes=60 * 1024 * 1024, collective_id=0, has_side_effects=True
        ),
    )(
        node_rows,
        cot_rows,
        wig,
        send,
        edge_src.reshape(1, LANES),
        dst,
        env,
        *weights,
    )
    updated, node_grad = pl.pallas_call(
        finish,
        out_shape=[rows16, rows16],
        in_specs=[anywhere] * 6 + [vmem] * 3,
        out_specs=[anywhere] * 2,
        scratch_shapes=[
            packed,
            pltpu.VMEM(wig.shape, BF16),
            atoms,
            pltpu.VMEM((flat, LANES), F32),
            ghost,
            ghost,
            pltpu.VMEM((8 * LANES, LANES), F32),
            atoms,
            atoms,
            atoms,
            pltpu.SemaphoreType.DMA((6,)),
            pltpu.SemaphoreType.DMA((3,)),
        ],
        compiler_params=pltpu.CompilerParams(vmem_limit_bytes=60 * 1024 * 1024),
    )(message, wig, node_rows, own_grad, below_grad, above_grad, send, dst, env)

    def restore(x):
        return jnp.transpose(x.reshape(NODE, 32, LANES), (2, 0, 1))

    return restore(updated), restore(node_grad)


def solution(mesh):
    in_specs = (
        P("space", None, "morder"),
        P("space"),
        P("space"),
        P("space"),
        P("space", None, None),
        P("space"),
        P(),
        P(),
        P(),
        P(),
        P(),
        P("space", None, "morder"),
    )
    out_specs = (P("space", None, "morder"), P("space", None, "morder"))
    return jax.shard_map(shards, mesh=mesh, in_specs=in_specs, out_specs=out_specs, check_vma=False)
```

```python
import jax
import jax.numpy as jnp
from jax import lax
from jax.experimental import pallas as pl
from jax.experimental.pallas import tpu as pltpu
from jax.sharding import PartitionSpec as P

F32, BF16 = jnp.float32, jnp.bfloat16
LANES = 128
HALF = 784
NODE = 49
EDGE = 29
PACKED = 240
PARTS = ((0, 6), (6, 6), (12, 5), (17, 5), (22, 7))


def degree_rows(degree):
    rows = [degree]
    if degree >= 1:
        rows += [6 + degree, 12 + degree]
    if degree >= 2:
        rows += [17 + degree, 22 + degree]
    return rows


def dot(a, b):
    return jnp.dot(a, b, preferred_element_type=F32)


def dot_t(a, b):
    return lax.dot_general(a, b, (((1,), (1,)), ((), ())), preferred_element_type=F32)


def one_hot(index_row, offset=0):
    rows = lax.broadcasted_iota(jnp.int32, (LANES, LANES), 0) + offset
    return jnp.where(rows == index_row, 1.0, 0.0).astype(F32)


def lane_low():
    return lax.broadcasted_iota(jnp.int32, (LANES, LANES), 1) < LANES // 2


def row_low():
    return lax.broadcasted_iota(jnp.int32, (LANES, LANES), 0) < LANES // 2


FIRST_ROWS = range(7, 19)
LATER_ROWS = tuple(range(19, 29)) + tuple(range(7))


def rotate(rot_ref, load, store, wanted):
    for degree in range(7):
        columns = range(degree * degree, (degree + 1) * (degree + 1))
        for k in degree_rows(degree):
            if k not in wanted:
                continue
            total = None
            for n in columns:
                term = rot_ref[n, k : k + 1, :].astype(F32) * load(n)
                total = term if total is None else total + term
            store(k, total)


def rotate_back(rot_ref, load, store):
    for degree in range(7):
        for n in range(degree * degree, (degree + 1) * (degree + 1)):
            total = None
            for k in degree_rows(degree):
                term = rot_ref[n, k : k + 1, :].astype(F32) * load(k)
                total = term if total is None else total + term
            store(n, total)


def place(k):
    return k - 7 if k >= 7 else k + 22


def channel_rows(n, count=1):
    return slice(n * 32, (n + count) * 32)


def swap_blocks(blocks):
    group = lax.broadcasted_iota(jnp.int32, blocks[0].shape, 1) // 32
    low = group < 2
    a0 = jnp.where(low, blocks[0], pltpu.roll(blocks[2], 64, 1))
    a2 = jnp.where(low, pltpu.roll(blocks[0], 64, 1), blocks[2])
    a1 = jnp.where(low, blocks[1], pltpu.roll(blocks[3], 64, 1))
    a3 = jnp.where(low, pltpu.roll(blocks[1], 64, 1), blocks[3])
    even = (group % 2) == 0
    b0 = jnp.where(even, a0, pltpu.roll(a1, 32, 1))
    b1 = jnp.where(even, pltpu.roll(a0, 96, 1), a1)
    b2 = jnp.where(even, a2, pltpu.roll(a3, 32, 1))
    b3 = jnp.where(even, pltpu.roll(a2, 96, 1), a3)
    return [b0, b1, b2, b3]


CHUNKS = ((0, 3), (3, 8))


def span_of(group):
    return slice(group * 32, min(group * 32 + 32, PACKED))


def fold(block):
    lane = lax.broadcasted_iota(jnp.int32, (16, LANES), 1)
    return jnp.where(lane < 32, block[:16], pltpu.roll(block[16:], 32, 1))


def unfold(block):
    return jnp.concatenate([block, pltpu.roll(block, 96, 1)], 0)


def store_transposed(rows_ref, out_ref, first, last):
    for group in range(first, last):
        piece = rows_ref[group * LANES : (group + 1) * LANES, :].T
        for part in range(4):
            block = piece[part * 32 : (part + 1) * 32]
            if group == 7:
                block = fold(block)
            out_ref[part, span_of(group)] = block.astype(BF16)


def load_group(in_ref, part, group):
    block = in_ref[part, span_of(group)].astype(F32)
    return unfold(block) if group == 7 else block


def load_transposed(in_ref, rows_ref, first, last):
    for group in range(first, last):
        piece = jnp.concatenate([load_group(in_ref, part, group) for part in range(4)], axis=0)
        rows_ref[group * LANES : (group + 1) * LANES, :] = piece.T


def piece_span(piece):
    first, last = CHUNKS[piece]
    return pl.ds(first * 32, min(last * 32, PACKED) - first * 32)


class Exchange:
    def __init__(self, send, recv, send_sem, recv_sem, base, kept_sem=None):
        self.send, self.recv = send, recv
        self.space, self.me = lax.axis_index("space"), lax.axis_index("morder")
        self.copies = {}
        self.kept = []
        for piece in range(len(CHUNKS)):
            if kept_sem is not None:
                span = piece_span(piece)
                self.kept.append(
                    pltpu.make_async_copy(send.at[self.me, span], recv.at[self.me, span], kept_sem.at[piece])
                )
            for step in (1, 2, 3):
                target = lax.rem(self.me + step, 4)
                slot = base + piece * 3 + step - 1
                span = piece_span(piece)
                self.copies[piece, step] = pltpu.make_async_remote_copy(
                    src_ref=send.at[target, span],
                    dst_ref=recv.at[self.me, span],
                    send_sem=send_sem.at[slot],
                    recv_sem=recv_sem.at[slot],
                    device_id=(self.space, target),
                    device_id_type=pl.DeviceIdType.MESH,
                )

    def start(self, piece):
        for step in (2, 1, 3):
            self.copies[piece, step].start()
        if self.kept:
            self.kept[piece].start()
        else:
            span = piece_span(piece)
            self.recv[self.me, span] = self.send[self.me, span]

    def arrived(self, piece):
        for step in (1, 2, 3):
            self.copies[piece, step].wait_recv()

    def sent(self):
        for copy in self.kept:
            copy.wait()
        for copy in self.copies.values():
            copy.wait_send()


def mirrored(blocks, far):
    return [jnp.where(far, blocks[3 - i], blocks[i]) for i in range(4)]


def map_edges(forward, before, after, weights, far):
    w_zero, w_one_real, w_one_imag, w_two_real, w_two_imag = weights
    product = dot if forward else dot_t
    blocks, results = [], []

    def take(piece):
        before.arrived(piece)
        for group in range(*CHUNKS[piece]):
            parts = [load_group(before.recv, i, group) for i in range(4)]
            blocks.extend(swap_blocks(mirrored(parts, far) if forward else parts))

    def part(i):
        start, count = PARTS[i]
        return jnp.concatenate(blocks[start : start + count], 1).astype(BF16)

    def put(value):
        results.extend(value[:, i * LANES : (i + 1) * LANES] for i in range(value.shape[1] // LANES))

    def pair(first, real, imag):
        both = jnp.concatenate([part(first), part(first + 1)], 0)
        straight = product(both, real[...])
        crossed = product(both, imag[...])
        if forward:
            put(straight[:32] - crossed[32:])
            put(straight[32:] + crossed[:32])
        else:
            put(straight[:32] + crossed[32:])
            put(straight[32:] - crossed[:32])

    def give(piece):
        for group in range(*CHUNKS[piece]):
            parts = swap_blocks(results[4 * group : 4 * group + 4])
            for i, value in enumerate(parts if forward else mirrored(parts, far)):
                if group == 7:
                    value = fold(value)
                after.send[i, span_of(group)] = value.astype(BF16)
        after.start(piece)

    take(0)
    pair(0, w_one_real, w_one_imag)
    give(0)
    take(1)
    pair(2, w_two_real, w_two_imag)
    put(product(part(4), w_zero[...]))
    results.extend([jnp.zeros_like(results[0])] * 3)
    give(1)


def ghost_pack(product, source, first, second, low, high):
    for row in range(0, HALF, 112):
        both = product(source[row : row + 112], first) + product(source[HALF + row : HALF + row + 112], second)
        both = both.astype(BF16)
        low[row : row + 112] = both[:, :LANES]
        high[row : row + 112] = both[:, LANES:]


def layer(
    nodes_hbm,
    cot_hbm,
    wig_hbm,
    send_ref,
    src_ref,
    dst_ref,
    env_ref,
    w0_hbm,
    w1r_hbm,
    w1i_hbm,
    w2r_hbm,
    w2i_hbm,
    msg_recv,
    own_hbm,
    below_grad,
    above_grad,
    nodes,
    cot,
    wig,
    w0,
    w1r,
    w1i,
    w2r,
    w2i,
    low,
    high,
    below,
    above,
    low_grad,
    high_grad,
    edge_send,
    edge_recv,
    back_send,
    back_recv,
    rot_send,
    rot_recv,
    msg_send,
    rows,
    hot,
    hot_half,
    own_grad,
    far_rows,
    local_sem,
    out_sem,
    kept_sem,
    send_sem,
    recv_sem,
    ghost_send_sem,
    ghost_recv_sem,
):
    space, me = lax.axis_index("space"), lax.axis_index("morder")
    domains = lax.axis_size("space")
    upper = lax.rem(space + 1, domains)
    lower = lax.rem(space + domains - 1, domains)
    odd = lax.rem(space, 2)
    mirror = 3 - 2 * me
    upper_place = me + odd * mirror
    lower_place = me + (1 - odd) * mirror
    peers = [(upper, upper_place), (lower, lower_place)] + [(space, lax.rem(me + step, 4)) for step in (1, 2, 3)]
    barrier = pltpu.get_barrier_semaphore()
    for peer in peers:
        pl.semaphore_signal(barrier, inc=1, device_id=peer, device_id_type=pl.DeviceIdType.MESH)
    loads = [
        pltpu.make_async_copy(a, b, local_sem.at[i])
        for i, (a, b) in enumerate(
            (
                (cot_hbm, cot),
                (wig_hbm, wig),
                (nodes_hbm, nodes),
                (w0_hbm, w0),
                (w1r_hbm, w1r),
                (w1i_hbm, w1i),
                (w2r_hbm, w2r),
                (w2i_hbm, w2i),
            )
        )
    ]
    for load in loads:
        load.start()
    weights = (w0, w1r, w1i, w2r, w2i)

    def ghost_copy(slot, source, target, device, position):
        return pltpu.make_async_remote_copy(
            src_ref=source,
            dst_ref=target,
            send_sem=ghost_send_sem.at[slot],
            recv_sem=ghost_recv_sem.at[slot],
            device_id=(device, position),
            device_id_type=pl.DeviceIdType.MESH,
        )

    ghosts = [
        ghost_copy(0, high, below, upper, upper_place),
        ghost_copy(1, low, above, lower, lower_place),
        ghost_copy(2, high_grad, below_grad, upper, upper_place),
        ghost_copy(3, low_grad, above_grad, lower, lower_place),
    ]
    pieces = len(CHUNKS) * 3
    edge_x = Exchange(edge_send, edge_recv, send_sem, recv_sem, 0)
    back_x = Exchange(back_send, back_recv, send_sem, recv_sem, pieces)
    rot_x = Exchange(rot_send, rot_recv, send_sem, recv_sem, 2 * pieces)
    msg_x = Exchange(msg_send, msg_recv, send_sem, recv_sem, 3 * pieces, kept_sem)

    side, rside = lane_low(), row_low()
    zero = jnp.zeros((LANES, LANES), F32)
    scale = env_ref[...]
    rows[EDGE * 32 :] = jnp.zeros((8 * LANES - EDGE * 32, LANES), F32)

    loads[0].wait()
    hot[...] = dot(cot[...], one_hot(dst_ref[...]).astype(BF16))
    loads[1].wait()

    def store_scaled(k, value):
        rows[channel_rows(place(k))] = value * scale

    def store_plain(k, value):
        rows[channel_rows(place(k))] = value

    for piece, (first, last) in enumerate(CHUNKS):
        rotate(wig, lambda n: hot[channel_rows(n)], store_scaled, (FIRST_ROWS, LATER_ROWS)[piece])
        store_transposed(rows, edge_send, first, last)
        if piece == 0:
            pl.semaphore_wait(barrier, len(peers))
        edge_x.start(piece)

    match = one_hot(send_ref[...])
    turned = pltpu.roll(match, 64, 1)
    loads[2].wait()
    ghost_pack(
        dot,
        nodes,
        jnp.concatenate([jnp.where(side, match, zero), jnp.where(side, zero, match)], 1).astype(BF16),
        jnp.concatenate([jnp.where(side, zero, turned), jnp.where(side, turned, zero)], 1).astype(BF16),
        low,
        high,
    )
    ghosts[0].start()
    ghosts[1].start()
    index = src_ref[...]
    own = one_hot(index).astype(BF16)
    plain = one_hot(index, LANES)
    up = one_hot(index, LANES + 64)
    down = one_hot(index, 64)
    hot[...] = dot(nodes[...], own)

    for load in loads[3:]:
        load.wait()
    first_far = LANES + 64 * odd
    is_far = jnp.where((index >= first_far) & (index < first_far + 64), 1.0, 0.0).astype(F32)
    far_rows[...] = jnp.broadcast_to(is_far, (LANES, LANES)).T
    far = far_rows[pl.ds(pl.multiple_of(me * 32, 32), 32)] > 0.5
    map_edges(False, edge_x, back_x, weights, far)

    ghosts[0].wait_recv()
    ghosts[1].wait_recv()
    hot[:HALF] += dot(below[...], jnp.where(rside, zero, down).astype(BF16)) + dot(
        above[...], jnp.where(rside, up, zero).astype(BF16)
    )
    hot[HALF:] += dot(below[...], jnp.where(rside, plain, zero).astype(BF16)) + dot(
        above[...], jnp.where(rside, zero, plain).astype(BF16)
    )
    for piece, (first, last) in enumerate(CHUNKS):
        rotate(wig, lambda n: hot[channel_rows(n)], store_plain, (FIRST_ROWS, LATER_ROWS)[piece])
        store_transposed(rows, rot_send, first, last)
        rot_x.start(piece)

    for piece, (first, last) in enumerate(CHUNKS):
        back_x.arrived(piece)
        load_transposed(back_recv, rows, first, last)

    def store_half(n, value):
        hot_half[channel_rows(n)] = value.astype(BF16)

    rotate_back(wig, lambda k: rows[channel_rows(place(k))], store_half)
    ghost_pack(
        dot_t,
        hot_half,
        jnp.concatenate([jnp.where(rside, plain, zero), jnp.where(rside, zero, plain)], 0).astype(BF16),
        jnp.concatenate([jnp.where(rside, zero, down), jnp.where(rside, up, zero)], 0).astype(BF16),
        low_grad,
        high_grad,
    )
    ghosts[2].start()
    ghosts[3].start()
    own_grad[...] = dot_t(hot_half[...], own) + cot[...].astype(F32)
    last_write = pltpu.make_async_copy(own_grad, own_hbm, out_sem.at[0])
    last_write.start()

    map_edges(True, rot_x, msg_x, weights, far_rows[pl.ds(pl.multiple_of(me * 32, 32), 32)] > 0.5)

    for piece in range(len(CHUNKS)):
        msg_x.arrived(piece)
    ghosts[2].wait_recv()
    ghosts[3].wait_recv()
    for x in (edge_x, back_x, rot_x, msg_x):
        x.sent()
    for copy in ghosts:
        copy.wait_send()
    last_write.wait()


def finish(
    msg_hbm,
    wig_hbm,
    nodes_hbm,
    own_hbm,
    below_hbm,
    above_hbm,
    send_ref,
    dst_ref,
    env_ref,
    updated_hbm,
    grad_hbm,
    msg,
    wig,
    nodes,
    own,
    below,
    above,
    rows,
    hot,
    updated,
    grad,
    sem,
    out_sem,
):
    loads = [
        pltpu.make_async_copy(a, b, sem.at[i])
        for i, (a, b) in enumerate(
            (
                (msg_hbm, msg),
                (wig_hbm, wig),
                (nodes_hbm, nodes),
                (above_hbm, above),
                (below_hbm, below),
                (own_hbm, own),
            )
        )
    ]
    for load in loads:
        load.start()
    match = one_hot(send_ref[...])
    turned = pltpu.roll(match, 64, 1)
    side = lane_low()
    zero = jnp.zeros((LANES, LANES), F32)
    pairs = (
        (jnp.where(side, turned, zero), jnp.where(side, zero, turned)),
        (jnp.where(side, zero, match), jnp.where(side, match, zero)),
    )
    target = one_hot(dst_ref[...]).astype(BF16)
    scale = env_ref[...]
    loads[0].wait()
    load_transposed(msg, rows, 0, 8)
    loads[1].wait()

    def store_message(n, value):
        hot[channel_rows(n)] = (value * scale).astype(BF16)

    rotate_back(wig, lambda k: rows[channel_rows(place(k))], store_message)
    loads[2].wait()
    updated[...] = (nodes[...].astype(F32) + dot_t(hot[...], target)).astype(BF16)
    writes = [pltpu.make_async_copy(updated, updated_hbm, out_sem.at[0])]
    writes[0].start()
    for load in loads[3:]:
        load.wait()
    for half, (for_above, for_below) in enumerate(pairs):
        span = pl.ds(half * HALF, HALF)
        total = dot_t(above[...], for_above.astype(BF16)) + dot_t(below[...], for_below.astype(BF16))
        grad[span] = (own[span] + total).astype(BF16)
        writes.append(pltpu.make_async_copy(grad.at[span], grad_hbm.at[span], out_sem.at[1 + half]))
        writes[-1].start()
    for write in writes:
        write.wait()


def shards(
    nodes,
    ghost_send,
    edge_src,
    edge_dst,
    wigner,
    envelope,
    w_zero,
    w_one_real,
    w_one_imag,
    w_two_real,
    w_two_imag,
    cotangent,
):
    flat = NODE * 32
    node_rows = jnp.transpose(nodes, (1, 2, 0)).reshape(flat, LANES)
    cot_rows = jnp.transpose(cotangent, (1, 2, 0)).reshape(flat, LANES)
    wig = jnp.transpose(wigner, (2, 1, 0))
    atoms = pltpu.VMEM((flat, LANES), BF16)
    ghost = pltpu.VMEM((HALF, LANES), BF16)
    packed = pltpu.VMEM((4, PACKED, LANES), BF16)
    weights = (w_zero, w_one_real, w_one_imag, w_two_real, w_two_imag)
    copies = 4 * 3 * len(CHUNKS)
    anywhere = pl.BlockSpec(memory_space=pltpu.HBM)
    vmem = pl.BlockSpec(memory_space=pltpu.VMEM)
    rows16 = jax.ShapeDtypeStruct((flat, LANES), BF16)
    rows32 = jax.ShapeDtypeStruct((flat, LANES), F32)
    returned = jax.ShapeDtypeStruct((HALF, LANES), BF16)
    send = ghost_send.reshape(1, LANES)
    dst = edge_dst.reshape(1, LANES)
    env = envelope.reshape(1, LANES)
    message, own_grad, below_grad, above_grad = pl.pallas_call(
        layer,
        out_shape=[jax.ShapeDtypeStruct((4, PACKED, LANES), BF16), rows32, returned, returned],
        in_specs=[anywhere] * 3 + [vmem] * 4 + [anywhere] * 5,
        out_specs=[anywhere] * 4,
        scratch_shapes=[atoms, atoms, pltpu.VMEM(wig.shape, BF16)]
        + [pltpu.VMEM(w.shape, BF16) for w in weights]
        + [ghost] * 6
        + [packed] * 7
        + [
            pltpu.VMEM((8 * LANES, LANES), F32),
            pltpu.VMEM((flat, LANES), F32),
            atoms,
            pltpu.VMEM((flat, LANES), F32),
            pltpu.VMEM((LANES, LANES), F32),
            pltpu.SemaphoreType.DMA((8,)),
            pltpu.SemaphoreType.DMA((1,)),
            pltpu.SemaphoreType.DMA((len(CHUNKS),)),
            pltpu.SemaphoreType.DMA((copies,)),
            pltpu.SemaphoreType.DMA((copies,)),
            pltpu.SemaphoreType.DMA((4,)),
            pltpu.SemaphoreType.DMA((4,)),
        ],
        compiler_params=pltpu.CompilerParams(
            vmem_limit_bytes=60 * 1024 * 1024, collective_id=0, has_side_effects=True
        ),
    )(
        node_rows,
        cot_rows,
        wig,
        send,
        edge_src.reshape(1, LANES),
        dst,
        env,
        *weights,
    )
    updated, node_grad = pl.pallas_call(
        finish,
        out_shape=[rows16, rows16],
        in_specs=[anywhere] * 6 + [vmem] * 3,
        out_specs=[anywhere] * 2,
        scratch_shapes=[
            packed,
            pltpu.VMEM(wig.shape, BF16),
            atoms,
            pltpu.VMEM((flat, LANES), F32),
            ghost,
            ghost,
            pltpu.VMEM((8 * LANES, LANES), F32),
            atoms,
            atoms,
            atoms,
            pltpu.SemaphoreType.DMA((6,)),
            pltpu.SemaphoreType.DMA((3,)),
        ],
        compiler_params=pltpu.CompilerParams(vmem_limit_bytes=60 * 1024 * 1024),
    )(message, wig, node_rows, own_grad, below_grad, above_grad, send, dst, env)

    def restore(x):
        return jnp.transpose(x.reshape(NODE, 32, LANES), (2, 0, 1))

    return restore(updated), restore(node_grad)


def solution(mesh):
    in_specs = (
        P("space", None, "morder"),
        P("space"),
        P("space"),
        P("space"),
        P("space", None, None),
        P("space"),
        P(),
        P(),
        P(),
        P(),
        P(),
        P("space", None, "morder"),
    )
    out_specs = (P("space", None, "morder"), P("space", None, "morder"))
    return jax.shard_map(shards, mesh=mesh, in_specs=in_specs, out_specs=out_specs, check_vma=False)
```

```python
import jax
import jax.numpy as jnp
from jax import lax
from jax.experimental import pallas as pl
from jax.experimental.pallas import tpu as pltpu
from jax.sharding import PartitionSpec as P

F32, BF16 = jnp.float32, jnp.bfloat16
LANES = 128
HALF = 784
NODE = 49
EDGE = 29
PACKED = 240
PARTS = ((0, 6), (6, 6), (12, 5), (17, 5), (22, 7))


def degree_rows(degree):
    rows = [degree]
    if degree >= 1:
        rows += [6 + degree, 12 + degree]
    if degree >= 2:
        rows += [17 + degree, 22 + degree]
    return rows


def dot(a, b):
    return jnp.dot(a, b, preferred_element_type=F32)


def dot_t(a, b):
    return lax.dot_general(a, b, (((1,), (1,)), ((), ())), preferred_element_type=F32)


def one_hot(index_row, offset=0):
    rows = lax.broadcasted_iota(jnp.int32, (LANES, LANES), 0) + offset
    return jnp.where(rows == index_row, 1.0, 0.0).astype(F32)


def lane_low():
    return lax.broadcasted_iota(jnp.int32, (LANES, LANES), 1) < LANES // 2


def row_low():
    return lax.broadcasted_iota(jnp.int32, (LANES, LANES), 0) < LANES // 2


FIRST_ROWS = range(7, 19)
LATER_ROWS = tuple(range(19, 29)) + tuple(range(7))


def rotate(rot_ref, load, store, wanted):
    for degree in range(7):
        columns = range(degree * degree, (degree + 1) * (degree + 1))
        for k in degree_rows(degree):
            if k not in wanted:
                continue
            total = None
            for n in columns:
                term = rot_ref[n, k : k + 1, :].astype(F32) * load(n)
                total = term if total is None else total + term
            store(k, total)


def rotate_back(rot_ref, load, store):
    for degree in range(7):
        for n in range(degree * degree, (degree + 1) * (degree + 1)):
            total = None
            for k in degree_rows(degree):
                term = rot_ref[n, k : k + 1, :].astype(F32) * load(k)
                total = term if total is None else total + term
            store(n, total)


def place(k):
    return k - 7 if k >= 7 else k + 22


def channel_rows(n, count=1):
    return slice(n * 32, (n + count) * 32)


def swap_blocks(blocks):
    group = lax.broadcasted_iota(jnp.int32, blocks[0].shape, 1) // 32
    low = group < 2
    a0 = jnp.where(low, blocks[0], pltpu.roll(blocks[2], 64, 1))
    a2 = jnp.where(low, pltpu.roll(blocks[0], 64, 1), blocks[2])
    a1 = jnp.where(low, blocks[1], pltpu.roll(blocks[3], 64, 1))
    a3 = jnp.where(low, pltpu.roll(blocks[1], 64, 1), blocks[3])
    even = (group % 2) == 0
    b0 = jnp.where(even, a0, pltpu.roll(a1, 32, 1))
    b1 = jnp.where(even, pltpu.roll(a0, 96, 1), a1)
    b2 = jnp.where(even, a2, pltpu.roll(a3, 32, 1))
    b3 = jnp.where(even, pltpu.roll(a2, 96, 1), a3)
    return [b0, b1, b2, b3]


CHUNKS = ((0, 3), (3, 8))


def span_of(group):
    return slice(group * 32, min(group * 32 + 32, PACKED))


def fold(block):
    lane = lax.broadcasted_iota(jnp.int32, (16, LANES), 1)
    return jnp.where(lane < 32, block[:16], pltpu.roll(block[16:], 32, 1))


def unfold(block):
    return jnp.concatenate([block, pltpu.roll(block, 96, 1)], 0)


def store_transposed(rows_ref, out_ref, first, last):
    for group in range(first, last):
        piece = rows_ref[group * LANES : (group + 1) * LANES, :].T
        for part in range(4):
            block = piece[part * 32 : (part + 1) * 32]
            if group == 7:
                block = fold(block)
            out_ref[part, span_of(group)] = block.astype(BF16)


def load_group(in_ref, part, group):
    block = in_ref[part, span_of(group)].astype(F32)
    return unfold(block) if group == 7 else block


def load_transposed(in_ref, rows_ref, first, last):
    for group in range(first, last):
        piece = jnp.concatenate([load_group(in_ref, part, group) for part in range(4)], axis=0)
        rows_ref[group * LANES : (group + 1) * LANES, :] = piece.T


def piece_span(piece):
    first, last = CHUNKS[piece]
    return pl.ds(first * 32, min(last * 32, PACKED) - first * 32)


class Exchange:
    def __init__(self, send, recv, send_sem, recv_sem, base, kept_sem=None):
        self.send, self.recv = send, recv
        self.space, self.me = lax.axis_index("space"), lax.axis_index("morder")
        self.copies = {}
        self.kept = []
        for piece in range(len(CHUNKS)):
            if kept_sem is not None:
                span = piece_span(piece)
                self.kept.append(
                    pltpu.make_async_copy(send.at[self.me, span], recv.at[self.me, span], kept_sem.at[piece])
                )
            for step in (1, 2, 3):
                target = lax.rem(self.me + step, 4)
                slot = base + piece * 3 + step - 1
                span = piece_span(piece)
                self.copies[piece, step] = pltpu.make_async_remote_copy(
                    src_ref=send.at[target, span],
                    dst_ref=recv.at[self.me, span],
                    send_sem=send_sem.at[slot],
                    recv_sem=recv_sem.at[slot],
                    device_id=(self.space, target),
                    device_id_type=pl.DeviceIdType.MESH,
                )

    def start(self, piece):
        for step in (2, 1, 3):
            self.copies[piece, step].start()
        if self.kept:
            self.kept[piece].start()
        else:
            span = piece_span(piece)
            self.recv[self.me, span] = self.send[self.me, span]

    def arrived(self, piece):
        for step in (1, 2, 3):
            self.copies[piece, step].wait_recv()

    def sent(self):
        for copy in self.kept:
            copy.wait()
        for copy in self.copies.values():
            copy.wait_send()


def mirrored(blocks, far):
    return [jnp.where(far, blocks[3 - i], blocks[i]) for i in range(4)]


def map_edges(forward, before, after, weights, far):
    w_zero, w_one_real, w_one_imag, w_two_real, w_two_imag = weights
    product = dot if forward else dot_t
    blocks, results = [], []

    def take(piece):
        before.arrived(piece)
        for group in range(*CHUNKS[piece]):
            parts = [load_group(before.recv, i, group) for i in range(4)]
            blocks.extend(swap_blocks(mirrored(parts, far) if forward else parts))

    def part(i):
        start, count = PARTS[i]
        return jnp.concatenate(blocks[start : start + count], 1).astype(BF16)

    def put(value):
        results.extend(value[:, i * LANES : (i + 1) * LANES] for i in range(value.shape[1] // LANES))

    def pair(first, real, imag):
        both = jnp.concatenate([part(first), part(first + 1)], 0)
        straight = product(both, real[...])
        crossed = product(both, imag[...])
        if forward:
            put(straight[:32] - crossed[32:])
            put(straight[32:] + crossed[:32])
        else:
            put(straight[:32] + crossed[32:])
            put(straight[32:] - crossed[:32])

    def give(piece):
        for group in range(*CHUNKS[piece]):
            parts = swap_blocks(results[4 * group : 4 * group + 4])
            for i, value in enumerate(parts if forward else mirrored(parts, far)):
                if group == 7:
                    value = fold(value)
                after.send[i, span_of(group)] = value.astype(BF16)
        after.start(piece)

    take(0)
    pair(0, w_one_real, w_one_imag)
    give(0)
    take(1)
    pair(2, w_two_real, w_two_imag)
    put(product(part(4), w_zero[...]))
    results.extend([jnp.zeros_like(results[0])] * 3)
    give(1)


def ghost_pack(product, source, first, second, low, high):
    for row in range(0, HALF, 112):
        both = product(source[row : row + 112], first) + product(source[HALF + row : HALF + row + 112], second)
        both = both.astype(BF16)
        low[row : row + 112] = both[:, :LANES]
        high[row : row + 112] = both[:, LANES:]


def layer(
    nodes_hbm,
    cot_hbm,
    wig_hbm,
    send_ref,
    src_ref,
    dst_ref,
    env_ref,
    w0_hbm,
    w1r_hbm,
    w1i_hbm,
    w2r_hbm,
    w2i_hbm,
    msg_recv,
    own_hbm,
    below_grad,
    above_grad,
    nodes,
    cot,
    wig,
    w0,
    w1r,
    w1i,
    w2r,
    w2i,
    low,
    high,
    below,
    above,
    low_grad,
    high_grad,
    edge_send,
    edge_recv,
    back_send,
    back_recv,
    rot_send,
    rot_recv,
    msg_send,
    rows,
    hot,
    hot_half,
    own_grad,
    far_rows,
    local_sem,
    out_sem,
    kept_sem,
    send_sem,
    recv_sem,
    ghost_send_sem,
    ghost_recv_sem,
):
    space, me = lax.axis_index("space"), lax.axis_index("morder")
    domains = lax.axis_size("space")
    upper = lax.rem(space + 1, domains)
    lower = lax.rem(space + domains - 1, domains)
    odd = lax.rem(space, 2)
    mirror = 3 - 2 * me
    upper_place = me + odd * mirror
    lower_place = me + (1 - odd) * mirror
    peers = [(upper, upper_place), (lower, lower_place)] + [(space, lax.rem(me + step, 4)) for step in (1, 2, 3)]
    barrier = pltpu.get_barrier_semaphore()
    for peer in peers:
        pl.semaphore_signal(barrier, inc=1, device_id=peer, device_id_type=pl.DeviceIdType.MESH)
    loads = [
        pltpu.make_async_copy(a, b, local_sem.at[i])
        for i, (a, b) in enumerate(
            (
                (cot_hbm, cot),
                (wig_hbm, wig),
                (nodes_hbm, nodes),
                (w0_hbm, w0),
                (w1r_hbm, w1r),
                (w1i_hbm, w1i),
                (w2r_hbm, w2r),
                (w2i_hbm, w2i),
            )
        )
    ]
    for load in loads[:3]:
        load.start()
    weights = (w0, w1r, w1i, w2r, w2i)

    def ghost_copy(slot, source, target, device, position):
        return pltpu.make_async_remote_copy(
            src_ref=source,
            dst_ref=target,
            send_sem=ghost_send_sem.at[slot],
            recv_sem=ghost_recv_sem.at[slot],
            device_id=(device, position),
            device_id_type=pl.DeviceIdType.MESH,
        )

    ghosts = [
        ghost_copy(0, high, below, upper, upper_place),
        ghost_copy(1, low, above, lower, lower_place),
        ghost_copy(2, high_grad, below_grad, upper, upper_place),
        ghost_copy(3, low_grad, above_grad, lower, lower_place),
    ]
    pieces = len(CHUNKS) * 3
    edge_x = Exchange(edge_send, edge_recv, send_sem, recv_sem, 0)
    back_x = Exchange(back_send, back_recv, send_sem, recv_sem, pieces)
    rot_x = Exchange(rot_send, rot_recv, send_sem, recv_sem, 2 * pieces)
    msg_x = Exchange(msg_send, msg_recv, send_sem, recv_sem, 3 * pieces, kept_sem)

    side, rside = lane_low(), row_low()
    zero = jnp.zeros((LANES, LANES), F32)
    scale = env_ref[...]
    rows[EDGE * 32 :] = jnp.zeros((8 * LANES - EDGE * 32, LANES), F32)

    loads[0].wait()
    hot[...] = dot(cot[...], one_hot(dst_ref[...]).astype(BF16))
    loads[1].wait()
    for load in loads[3:]:
        load.start()

    def store_scaled(k, value):
        rows[channel_rows(place(k))] = value * scale

    def store_plain(k, value):
        rows[channel_rows(place(k))] = value

    def pack():
        match = one_hot(send_ref[...])
        turned = pltpu.roll(match, 64, 1)
        ghost_pack(
            dot,
            nodes,
            jnp.concatenate([jnp.where(side, match, zero), jnp.where(side, zero, match)], 1).astype(BF16),
            jnp.concatenate([jnp.where(side, zero, turned), jnp.where(side, turned, zero)], 1).astype(BF16),
            low,
            high,
        )

    for piece, (first, last) in enumerate(CHUNKS):
        rotate(wig, lambda n: hot[channel_rows(n)], store_scaled, (FIRST_ROWS, LATER_ROWS)[piece])
        store_transposed(rows, edge_send, first, last)
        if piece == 0:
            loads[2].wait()
            pack()
            pl.semaphore_wait(barrier, len(peers))
        edge_x.start(piece)
        if piece == 0:
            ghosts[0].start()
            ghosts[1].start()

    index = src_ref[...]
    own = one_hot(index).astype(BF16)
    plain = one_hot(index, LANES)
    up = one_hot(index, LANES + 64)
    down = one_hot(index, 64)
    hot[...] = dot(nodes[...], own)

    for load in loads[3:]:
        load.wait()
    first_far = LANES + 64 * odd
    is_far = jnp.where((index >= first_far) & (index < first_far + 64), 1.0, 0.0).astype(F32)
    far_rows[...] = jnp.broadcast_to(is_far, (LANES, LANES)).T
    far = far_rows[pl.ds(pl.multiple_of(me * 32, 32), 32)] > 0.5
    map_edges(False, edge_x, back_x, weights, far)

    ghosts[0].wait_recv()
    ghosts[1].wait_recv()
    hot[:HALF] += dot(below[...], jnp.where(rside, zero, down).astype(BF16)) + dot(
        above[...], jnp.where(rside, up, zero).astype(BF16)
    )
    hot[HALF:] += dot(below[...], jnp.where(rside, plain, zero).astype(BF16)) + dot(
        above[...], jnp.where(rside, zero, plain).astype(BF16)
    )
    for piece, (first, last) in enumerate(CHUNKS):
        rotate(wig, lambda n: hot[channel_rows(n)], store_plain, (FIRST_ROWS, LATER_ROWS)[piece])
        store_transposed(rows, rot_send, first, last)
        rot_x.start(piece)

    for piece, (first, last) in enumerate(CHUNKS):
        back_x.arrived(piece)
        load_transposed(back_recv, rows, first, last)

    def store_half(n, value):
        hot_half[channel_rows(n)] = value.astype(BF16)

    rotate_back(wig, lambda k: rows[channel_rows(place(k))], store_half)
    ghost_pack(
        dot_t,
        hot_half,
        jnp.concatenate([jnp.where(rside, plain, zero), jnp.where(rside, zero, plain)], 0).astype(BF16),
        jnp.concatenate([jnp.where(rside, zero, down), jnp.where(rside, up, zero)], 0).astype(BF16),
        low_grad,
        high_grad,
    )
    ghosts[2].start()
    ghosts[3].start()
    own_grad[...] = dot_t(hot_half[...], own) + cot[...].astype(F32)
    last_write = pltpu.make_async_copy(own_grad, own_hbm, out_sem.at[0])
    last_write.start()

    map_edges(True, rot_x, msg_x, weights, far_rows[pl.ds(pl.multiple_of(me * 32, 32), 32)] > 0.5)

    for piece in range(len(CHUNKS)):
        msg_x.arrived(piece)
    ghosts[2].wait_recv()
    ghosts[3].wait_recv()
    for x in (edge_x, back_x, rot_x, msg_x):
        x.sent()
    for copy in ghosts:
        copy.wait_send()
    last_write.wait()


def finish(
    msg_hbm,
    wig_hbm,
    nodes_hbm,
    own_hbm,
    below_hbm,
    above_hbm,
    send_ref,
    dst_ref,
    env_ref,
    updated_hbm,
    grad_hbm,
    msg,
    wig,
    nodes,
    own,
    below,
    above,
    rows,
    hot,
    updated,
    grad,
    sem,
    out_sem,
):
    loads = [
        pltpu.make_async_copy(a, b, sem.at[i])
        for i, (a, b) in enumerate(
            (
                (msg_hbm, msg),
                (wig_hbm, wig),
                (nodes_hbm, nodes),
                (above_hbm, above),
                (below_hbm, below),
                (own_hbm, own),
            )
        )
    ]
    for load in loads:
        load.start()
    match = one_hot(send_ref[...])
    turned = pltpu.roll(match, 64, 1)
    side = lane_low()
    zero = jnp.zeros((LANES, LANES), F32)
    pairs = (
        (jnp.where(side, turned, zero), jnp.where(side, zero, turned)),
        (jnp.where(side, zero, match), jnp.where(side, match, zero)),
    )
    target = one_hot(dst_ref[...]).astype(BF16)
    scale = env_ref[...]
    loads[0].wait()
    load_transposed(msg, rows, 0, 8)
    loads[1].wait()

    def store_message(n, value):
        hot[channel_rows(n)] = (value * scale).astype(BF16)

    rotate_back(wig, lambda k: rows[channel_rows(place(k))], store_message)
    loads[2].wait()
    updated[...] = (nodes[...].astype(F32) + dot_t(hot[...], target)).astype(BF16)
    writes = [pltpu.make_async_copy(updated, updated_hbm, out_sem.at[0])]
    writes[0].start()
    for load in loads[3:]:
        load.wait()
    for half, (for_above, for_below) in enumerate(pairs):
        span = pl.ds(half * HALF, HALF)
        total = dot_t(above[...], for_above.astype(BF16)) + dot_t(below[...], for_below.astype(BF16))
        grad[span] = (own[span] + total).astype(BF16)
        writes.append(pltpu.make_async_copy(grad.at[span], grad_hbm.at[span], out_sem.at[1 + half]))
        writes[-1].start()
    for write in writes:
        write.wait()


def shards(
    nodes,
    ghost_send,
    edge_src,
    edge_dst,
    wigner,
    envelope,
    w_zero,
    w_one_real,
    w_one_imag,
    w_two_real,
    w_two_imag,
    cotangent,
):
    flat = NODE * 32
    node_rows = jnp.transpose(nodes, (1, 2, 0)).reshape(flat, LANES)
    cot_rows = jnp.transpose(cotangent, (1, 2, 0)).reshape(flat, LANES)
    wig = jnp.transpose(wigner, (2, 1, 0))
    atoms = pltpu.VMEM((flat, LANES), BF16)
    ghost = pltpu.VMEM((HALF, LANES), BF16)
    packed = pltpu.VMEM((4, PACKED, LANES), BF16)
    weights = (w_zero, w_one_real, w_one_imag, w_two_real, w_two_imag)
    copies = 4 * 3 * len(CHUNKS)
    anywhere = pl.BlockSpec(memory_space=pltpu.HBM)
    vmem = pl.BlockSpec(memory_space=pltpu.VMEM)
    rows16 = jax.ShapeDtypeStruct((flat, LANES), BF16)
    rows32 = jax.ShapeDtypeStruct((flat, LANES), F32)
    returned = jax.ShapeDtypeStruct((HALF, LANES), BF16)
    send = ghost_send.reshape(1, LANES)
    dst = edge_dst.reshape(1, LANES)
    env = envelope.reshape(1, LANES)
    message, own_grad, below_grad, above_grad = pl.pallas_call(
        layer,
        out_shape=[jax.ShapeDtypeStruct((4, PACKED, LANES), BF16), rows32, returned, returned],
        in_specs=[anywhere] * 3 + [vmem] * 4 + [anywhere] * 5,
        out_specs=[anywhere] * 4,
        scratch_shapes=[atoms, atoms, pltpu.VMEM(wig.shape, BF16)]
        + [pltpu.VMEM(w.shape, BF16) for w in weights]
        + [ghost] * 6
        + [packed] * 7
        + [
            pltpu.VMEM((8 * LANES, LANES), F32),
            pltpu.VMEM((flat, LANES), F32),
            atoms,
            pltpu.VMEM((flat, LANES), F32),
            pltpu.VMEM((LANES, LANES), F32),
            pltpu.SemaphoreType.DMA((8,)),
            pltpu.SemaphoreType.DMA((1,)),
            pltpu.SemaphoreType.DMA((len(CHUNKS),)),
            pltpu.SemaphoreType.DMA((copies,)),
            pltpu.SemaphoreType.DMA((copies,)),
            pltpu.SemaphoreType.DMA((4,)),
            pltpu.SemaphoreType.DMA((4,)),
        ],
        compiler_params=pltpu.CompilerParams(
            vmem_limit_bytes=60 * 1024 * 1024, collective_id=0, has_side_effects=True
        ),
    )(
        node_rows,
        cot_rows,
        wig,
        send,
        edge_src.reshape(1, LANES),
        dst,
        env,
        *weights,
    )
    updated, node_grad = pl.pallas_call(
        finish,
        out_shape=[rows16, rows16],
        in_specs=[anywhere] * 6 + [vmem] * 3,
        out_specs=[anywhere] * 2,
        scratch_shapes=[
            packed,
            pltpu.VMEM(wig.shape, BF16),
            atoms,
            pltpu.VMEM((flat, LANES), F32),
            ghost,
            ghost,
            pltpu.VMEM((8 * LANES, LANES), F32),
            atoms,
            atoms,
            atoms,
            pltpu.SemaphoreType.DMA((6,)),
            pltpu.SemaphoreType.DMA((3,)),
        ],
        compiler_params=pltpu.CompilerParams(vmem_limit_bytes=60 * 1024 * 1024),
    )(message, wig, node_rows, own_grad, below_grad, above_grad, send, dst, env)

    def restore(x):
        return jnp.transpose(x.reshape(NODE, 32, LANES), (2, 0, 1))

    return restore(updated), restore(node_grad)


def solution(mesh):
    in_specs = (
        P("space", None, "morder"),
        P("space"),
        P("space"),
        P("space"),
        P("space", None, None),
        P("space"),
        P(),
        P(),
        P(),
        P(),
        P(),
        P("space", None, "morder"),
    )
    out_specs = (P("space", None, "morder"), P("space", None, "morder"))
    return jax.shard_map(shards, mesh=mesh, in_specs=in_specs, out_specs=out_specs, check_vma=False)
```

```python
import jax
import jax.numpy as jnp
from jax import lax
from jax.experimental import pallas as pl
from jax.experimental.pallas import tpu as pltpu
from jax.sharding import PartitionSpec as P

F32, BF16 = jnp.float32, jnp.bfloat16
LANES = 128
HALF = 784
NODE = 49
EDGE = 29
PACKED = 240
PARTS = ((0, 6), (6, 6), (12, 5), (17, 5), (22, 7))


def degree_rows(degree):
    rows = [degree]
    if degree >= 1:
        rows += [6 + degree, 12 + degree]
    if degree >= 2:
        rows += [17 + degree, 22 + degree]
    return rows


def dot(a, b):
    return jnp.dot(a, b, preferred_element_type=F32)


def dot_t(a, b):
    return lax.dot_general(a, b, (((1,), (1,)), ((), ())), preferred_element_type=F32)


def one_hot(index_row, offset=0):
    rows = lax.broadcasted_iota(jnp.int32, (LANES, LANES), 0) + offset
    return jnp.where(rows == index_row, 1.0, 0.0).astype(F32)


def lane_low():
    return lax.broadcasted_iota(jnp.int32, (LANES, LANES), 1) < LANES // 2


def row_low():
    return lax.broadcasted_iota(jnp.int32, (LANES, LANES), 0) < LANES // 2


FIRST_ROWS = range(7, 19)
LATER_ROWS = tuple(range(19, 29)) + tuple(range(7))


def rotate(rot_ref, load, store, wanted):
    for degree in range(7):
        columns = range(degree * degree, (degree + 1) * (degree + 1))
        for k in degree_rows(degree):
            if k not in wanted:
                continue
            total = None
            for n in columns:
                term = rot_ref[n, k : k + 1, :].astype(F32) * load(n)
                total = term if total is None else total + term
            store(k, total)


def rotate_back(rot_ref, load, store):
    for degree in range(7):
        for n in range(degree * degree, (degree + 1) * (degree + 1)):
            total = None
            for k in degree_rows(degree):
                term = rot_ref[n, k : k + 1, :].astype(F32) * load(k)
                total = term if total is None else total + term
            store(n, total)


def place(k):
    return k - 7 if k >= 7 else k + 22


def channel_rows(n, count=1):
    return slice(n * 32, (n + count) * 32)


def swap_blocks(blocks):
    group = lax.broadcasted_iota(jnp.int32, blocks[0].shape, 1) // 32
    low = group < 2
    a0 = jnp.where(low, blocks[0], pltpu.roll(blocks[2], 64, 1))
    a2 = jnp.where(low, pltpu.roll(blocks[0], 64, 1), blocks[2])
    a1 = jnp.where(low, blocks[1], pltpu.roll(blocks[3], 64, 1))
    a3 = jnp.where(low, pltpu.roll(blocks[1], 64, 1), blocks[3])
    even = (group % 2) == 0
    b0 = jnp.where(even, a0, pltpu.roll(a1, 32, 1))
    b1 = jnp.where(even, pltpu.roll(a0, 96, 1), a1)
    b2 = jnp.where(even, a2, pltpu.roll(a3, 32, 1))
    b3 = jnp.where(even, pltpu.roll(a2, 96, 1), a3)
    return [b0, b1, b2, b3]


CHUNKS = ((0, 3), (3, 8))


def span_of(group):
    return slice(group * 32, min(group * 32 + 32, PACKED))


def fold(block):
    lane = lax.broadcasted_iota(jnp.int32, (16, LANES), 1)
    return jnp.where(lane < 32, block[:16], pltpu.roll(block[16:], 32, 1))


def unfold(block):
    return jnp.concatenate([block, pltpu.roll(block, 96, 1)], 0)


def store_transposed(rows_ref, out_ref, first, last):
    for group in range(first, last):
        piece = rows_ref[group * LANES : (group + 1) * LANES, :].T
        for part in range(4):
            block = piece[part * 32 : (part + 1) * 32]
            if group == 7:
                block = fold(block)
            out_ref[part, span_of(group)] = block.astype(BF16)


def load_group(in_ref, part, group):
    block = in_ref[part, span_of(group)].astype(F32)
    return unfold(block) if group == 7 else block


def load_transposed(in_ref, rows_ref, first, last):
    for group in range(first, last):
        piece = jnp.concatenate([load_group(in_ref, part, group) for part in range(4)], axis=0)
        rows_ref[group * LANES : (group + 1) * LANES, :] = piece.T


def piece_span(piece):
    first, last = CHUNKS[piece]
    return pl.ds(first * 32, min(last * 32, PACKED) - first * 32)


class Exchange:
    def __init__(self, send, recv, send_sem, recv_sem, base, kept_sem=None):
        self.send, self.recv = send, recv
        self.space, self.me = lax.axis_index("space"), lax.axis_index("morder")
        self.copies = {}
        self.kept = []
        for piece in range(len(CHUNKS)):
            if kept_sem is not None:
                span = piece_span(piece)
                self.kept.append(
                    pltpu.make_async_copy(send.at[self.me, span], recv.at[self.me, span], kept_sem.at[piece])
                )
            for step in (1, 2, 3):
                target = lax.rem(self.me + step, 4)
                slot = base + piece * 3 + step - 1
                span = piece_span(piece)
                self.copies[piece, step] = pltpu.make_async_remote_copy(
                    src_ref=send.at[target, span],
                    dst_ref=recv.at[self.me, span],
                    send_sem=send_sem.at[slot],
                    recv_sem=recv_sem.at[slot],
                    device_id=(self.space, target),
                    device_id_type=pl.DeviceIdType.MESH,
                )

    def start(self, piece):
        for step in (2, 1, 3):
            self.copies[piece, step].start()
        if self.kept:
            self.kept[piece].start()
        else:
            span = piece_span(piece)
            self.recv[self.me, span] = self.send[self.me, span]

    def arrived(self, piece):
        for step in (1, 2, 3):
            self.copies[piece, step].wait_recv()

    def sent(self):
        for copy in self.kept:
            copy.wait()
        for copy in self.copies.values():
            copy.wait_send()


def mirrored(blocks, far):
    return [jnp.where(far, blocks[3 - i], blocks[i]) for i in range(4)]


def map_edges(forward, before, after, weights, far):
    w_zero, w_one_real, w_one_imag, w_two_real, w_two_imag = weights
    product = dot if forward else dot_t
    blocks, results = [], []

    def take(piece):
        before.arrived(piece)
        for group in range(*CHUNKS[piece]):
            parts = [load_group(before.recv, i, group) for i in range(4)]
            blocks.extend(swap_blocks(mirrored(parts, far) if forward else parts))

    def part(i):
        start, count = PARTS[i]
        return jnp.concatenate(blocks[start : start + count], 1).astype(BF16)

    def put(value):
        results.extend(value[:, i * LANES : (i + 1) * LANES] for i in range(value.shape[1] // LANES))

    def pair(first, real, imag):
        both = jnp.concatenate([part(first), part(first + 1)], 0)
        straight = product(both, real[...])
        crossed = product(both, imag[...])
        if forward:
            put(straight[:32] - crossed[32:])
            put(straight[32:] + crossed[:32])
        else:
            put(straight[:32] + crossed[32:])
            put(straight[32:] - crossed[:32])

    def give(piece):
        for group in range(*CHUNKS[piece]):
            parts = swap_blocks(results[4 * group : 4 * group + 4])
            for i, value in enumerate(parts if forward else mirrored(parts, far)):
                if group == 7:
                    value = fold(value)
                after.send[i, span_of(group)] = value.astype(BF16)
        after.start(piece)

    take(0)
    pair(0, w_one_real, w_one_imag)
    give(0)
    take(1)
    pair(2, w_two_real, w_two_imag)
    put(product(part(4), w_zero[...]))
    results.extend([jnp.zeros_like(results[0])] * 3)
    give(1)


def ghost_pack(product, source, first, second, low, high):
    for row in range(0, HALF, 112):
        both = product(source[row : row + 112], first) + product(source[HALF + row : HALF + row + 112], second)
        both = both.astype(BF16)
        low[row : row + 112] = both[:, :LANES]
        high[row : row + 112] = both[:, LANES:]


def layer(
    nodes_hbm,
    cot_hbm,
    wig_hbm,
    send_ref,
    src_ref,
    dst_ref,
    env_ref,
    w0_hbm,
    w1r_hbm,
    w1i_hbm,
    w2r_hbm,
    w2i_hbm,
    msg_recv,
    own_hbm,
    below_grad,
    above_grad,
    nodes,
    cot,
    wig,
    w0,
    w1r,
    w1i,
    w2r,
    w2i,
    low,
    high,
    below,
    above,
    low_grad,
    high_grad,
    edge_send,
    edge_recv,
    back_send,
    back_recv,
    rot_send,
    rot_recv,
    msg_send,
    rows,
    hot,
    hot_half,
    own_grad,
    far_rows,
    local_sem,
    out_sem,
    kept_sem,
    send_sem,
    recv_sem,
    ghost_send_sem,
    ghost_recv_sem,
):
    space, me = lax.axis_index("space"), lax.axis_index("morder")
    domains = lax.axis_size("space")
    upper = lax.rem(space + 1, domains)
    lower = lax.rem(space + domains - 1, domains)
    odd = lax.rem(space, 2)
    mirror = 3 - 2 * me
    upper_place = me + odd * mirror
    lower_place = me + (1 - odd) * mirror
    peers = [(upper, upper_place), (lower, lower_place)] + [(space, lax.rem(me + step, 4)) for step in (1, 2, 3)]
    barrier = pltpu.get_barrier_semaphore()
    for peer in peers:
        pl.semaphore_signal(barrier, inc=1, device_id=peer, device_id_type=pl.DeviceIdType.MESH)
    loads = [
        pltpu.make_async_copy(a, b, local_sem.at[i])
        for i, (a, b) in enumerate(
            (
                (cot_hbm, cot),
                (wig_hbm, wig),
                (nodes_hbm, nodes),
                (w0_hbm, w0),
                (w1r_hbm, w1r),
                (w1i_hbm, w1i),
                (w2r_hbm, w2r),
                (w2i_hbm, w2i),
            )
        )
    ]
    for load in loads[:3]:
        load.start()
    weights = (w0, w1r, w1i, w2r, w2i)

    def ghost_copy(slot, source, target, device, position):
        return pltpu.make_async_remote_copy(
            src_ref=source,
            dst_ref=target,
            send_sem=ghost_send_sem.at[slot],
            recv_sem=ghost_recv_sem.at[slot],
            device_id=(device, position),
            device_id_type=pl.DeviceIdType.MESH,
        )

    ghosts = [
        ghost_copy(0, high, below, upper, upper_place),
        ghost_copy(1, low, above, lower, lower_place),
        ghost_copy(2, high_grad, below_grad, upper, upper_place),
        ghost_copy(3, low_grad, above_grad, lower, lower_place),
    ]
    pieces = len(CHUNKS) * 3
    edge_x = Exchange(edge_send, edge_recv, send_sem, recv_sem, 0)
    back_x = Exchange(back_send, back_recv, send_sem, recv_sem, pieces)
    rot_x = Exchange(rot_send, rot_recv, send_sem, recv_sem, 2 * pieces)
    msg_x = Exchange(msg_send, msg_recv, send_sem, recv_sem, 3 * pieces, kept_sem)

    side, rside = lane_low(), row_low()
    zero = jnp.zeros((LANES, LANES), F32)
    scale = env_ref[...]
    rows[EDGE * 32 :] = jnp.zeros((8 * LANES - EDGE * 32, LANES), F32)

    loads[0].wait()
    hot[...] = dot(cot[...], one_hot(dst_ref[...]).astype(BF16))
    loads[1].wait()
    for load in loads[3:]:
        load.start()

    def store_scaled(k, value):
        rows[channel_rows(place(k))] = value * scale

    def store_plain(k, value):
        rows[channel_rows(place(k))] = value

    def pack():
        match = one_hot(send_ref[...])
        turned = pltpu.roll(match, 64, 1)
        ghost_pack(
            dot,
            nodes,
            jnp.concatenate([jnp.where(side, match, zero), jnp.where(side, zero, match)], 1).astype(BF16),
            jnp.concatenate([jnp.where(side, zero, turned), jnp.where(side, turned, zero)], 1).astype(BF16),
            low,
            high,
        )

    for piece, (first, last) in enumerate(CHUNKS):
        rotate(wig, lambda n: hot[channel_rows(n)], store_scaled, (FIRST_ROWS, LATER_ROWS)[piece])
        store_transposed(rows, edge_send, first, last)
    loads[2].wait()
    pack()
    pl.semaphore_wait(barrier, len(peers))
    edge_x.start(0)
    ghosts[0].start()
    ghosts[1].start()
    edge_x.start(1)

    index = src_ref[...]
    own = one_hot(index).astype(BF16)
    plain = one_hot(index, LANES)
    up = one_hot(index, LANES + 64)
    down = one_hot(index, 64)
    hot[...] = dot(nodes[...], own)

    for load in loads[3:]:
        load.wait()
    first_far = LANES + 64 * odd
    is_far = jnp.where((index >= first_far) & (index < first_far + 64), 1.0, 0.0).astype(F32)
    far_rows[...] = jnp.broadcast_to(is_far, (LANES, LANES)).T
    far = far_rows[pl.ds(pl.multiple_of(me * 32, 32), 32)] > 0.5
    map_edges(False, edge_x, back_x, weights, far)

    ghosts[0].wait_recv()
    ghosts[1].wait_recv()
    hot[:HALF] += dot(below[...], jnp.where(rside, zero, down).astype(BF16)) + dot(
        above[...], jnp.where(rside, up, zero).astype(BF16)
    )
    hot[HALF:] += dot(below[...], jnp.where(rside, plain, zero).astype(BF16)) + dot(
        above[...], jnp.where(rside, zero, plain).astype(BF16)
    )
    for piece, (first, last) in enumerate(CHUNKS):
        rotate(wig, lambda n: hot[channel_rows(n)], store_plain, (FIRST_ROWS, LATER_ROWS)[piece])
        store_transposed(rows, rot_send, first, last)
        rot_x.start(piece)

    for piece, (first, last) in enumerate(CHUNKS):
        back_x.arrived(piece)
        load_transposed(back_recv, rows, first, last)

    def store_half(n, value):
        hot_half[channel_rows(n)] = value.astype(BF16)

    rotate_back(wig, lambda k: rows[channel_rows(place(k))], store_half)
    ghost_pack(
        dot_t,
        hot_half,
        jnp.concatenate([jnp.where(rside, plain, zero), jnp.where(rside, zero, plain)], 0).astype(BF16),
        jnp.concatenate([jnp.where(rside, zero, down), jnp.where(rside, up, zero)], 0).astype(BF16),
        low_grad,
        high_grad,
    )
    ghosts[2].start()
    ghosts[3].start()
    own_grad[...] = dot_t(hot_half[...], own) + cot[...].astype(F32)
    last_write = pltpu.make_async_copy(own_grad, own_hbm, out_sem.at[0])
    last_write.start()

    map_edges(True, rot_x, msg_x, weights, far_rows[pl.ds(pl.multiple_of(me * 32, 32), 32)] > 0.5)

    for piece in range(len(CHUNKS)):
        msg_x.arrived(piece)
    ghosts[2].wait_recv()
    ghosts[3].wait_recv()
    for x in (edge_x, back_x, rot_x, msg_x):
        x.sent()
    for copy in ghosts:
        copy.wait_send()
    last_write.wait()


def finish(
    msg_hbm,
    wig_hbm,
    nodes_hbm,
    own_hbm,
    below_hbm,
    above_hbm,
    send_ref,
    dst_ref,
    env_ref,
    updated_hbm,
    grad_hbm,
    msg,
    wig,
    nodes,
    own,
    below,
    above,
    rows,
    hot,
    updated,
    grad,
    sem,
    out_sem,
):
    loads = [
        pltpu.make_async_copy(a, b, sem.at[i])
        for i, (a, b) in enumerate(
            (
                (msg_hbm, msg),
                (wig_hbm, wig),
                (nodes_hbm, nodes),
                (above_hbm, above),
                (below_hbm, below),
                (own_hbm, own),
            )
        )
    ]
    for load in loads:
        load.start()
    match = one_hot(send_ref[...])
    turned = pltpu.roll(match, 64, 1)
    side = lane_low()
    zero = jnp.zeros((LANES, LANES), F32)
    pairs = (
        (jnp.where(side, turned, zero), jnp.where(side, zero, turned)),
        (jnp.where(side, zero, match), jnp.where(side, match, zero)),
    )
    target = one_hot(dst_ref[...]).astype(BF16)
    scale = env_ref[...]
    loads[0].wait()
    load_transposed(msg, rows, 0, 8)
    loads[1].wait()

    def store_message(n, value):
        hot[channel_rows(n)] = (value * scale).astype(BF16)

    rotate_back(wig, lambda k: rows[channel_rows(place(k))], store_message)
    loads[2].wait()
    updated[...] = (nodes[...].astype(F32) + dot_t(hot[...], target)).astype(BF16)
    writes = [pltpu.make_async_copy(updated, updated_hbm, out_sem.at[0])]
    writes[0].start()
    for load in loads[3:]:
        load.wait()
    for half, (for_above, for_below) in enumerate(pairs):
        span = pl.ds(half * HALF, HALF)
        total = dot_t(above[...], for_above.astype(BF16)) + dot_t(below[...], for_below.astype(BF16))
        grad[span] = (own[span] + total).astype(BF16)
        writes.append(pltpu.make_async_copy(grad.at[span], grad_hbm.at[span], out_sem.at[1 + half]))
        writes[-1].start()
    for write in writes:
        write.wait()


def shards(
    nodes,
    ghost_send,
    edge_src,
    edge_dst,
    wigner,
    envelope,
    w_zero,
    w_one_real,
    w_one_imag,
    w_two_real,
    w_two_imag,
    cotangent,
):
    flat = NODE * 32
    node_rows = jnp.transpose(nodes, (1, 2, 0)).reshape(flat, LANES)
    cot_rows = jnp.transpose(cotangent, (1, 2, 0)).reshape(flat, LANES)
    wig = jnp.transpose(wigner, (2, 1, 0))
    atoms = pltpu.VMEM((flat, LANES), BF16)
    ghost = pltpu.VMEM((HALF, LANES), BF16)
    packed = pltpu.VMEM((4, PACKED, LANES), BF16)
    weights = (w_zero, w_one_real, w_one_imag, w_two_real, w_two_imag)
    copies = 4 * 3 * len(CHUNKS)
    anywhere = pl.BlockSpec(memory_space=pltpu.HBM)
    vmem = pl.BlockSpec(memory_space=pltpu.VMEM)
    rows16 = jax.ShapeDtypeStruct((flat, LANES), BF16)
    rows32 = jax.ShapeDtypeStruct((flat, LANES), F32)
    returned = jax.ShapeDtypeStruct((HALF, LANES), BF16)
    send = ghost_send.reshape(1, LANES)
    dst = edge_dst.reshape(1, LANES)
    env = envelope.reshape(1, LANES)
    message, own_grad, below_grad, above_grad = pl.pallas_call(
        layer,
        out_shape=[jax.ShapeDtypeStruct((4, PACKED, LANES), BF16), rows32, returned, returned],
        in_specs=[anywhere] * 3 + [vmem] * 4 + [anywhere] * 5,
        out_specs=[anywhere] * 4,
        scratch_shapes=[atoms, atoms, pltpu.VMEM(wig.shape, BF16)]
        + [pltpu.VMEM(w.shape, BF16) for w in weights]
        + [ghost] * 6
        + [packed] * 7
        + [
            pltpu.VMEM((8 * LANES, LANES), F32),
            pltpu.VMEM((flat, LANES), F32),
            atoms,
            pltpu.VMEM((flat, LANES), F32),
            pltpu.VMEM((LANES, LANES), F32),
            pltpu.SemaphoreType.DMA((8,)),
            pltpu.SemaphoreType.DMA((1,)),
            pltpu.SemaphoreType.DMA((len(CHUNKS),)),
            pltpu.SemaphoreType.DMA((copies,)),
            pltpu.SemaphoreType.DMA((copies,)),
            pltpu.SemaphoreType.DMA((4,)),
            pltpu.SemaphoreType.DMA((4,)),
        ],
        compiler_params=pltpu.CompilerParams(
            vmem_limit_bytes=60 * 1024 * 1024, collective_id=0, has_side_effects=True
        ),
    )(
        node_rows,
        cot_rows,
        wig,
        send,
        edge_src.reshape(1, LANES),
        dst,
        env,
        *weights,
    )
    updated, node_grad = pl.pallas_call(
        finish,
        out_shape=[rows16, rows16],
        in_specs=[anywhere] * 6 + [vmem] * 3,
        out_specs=[anywhere] * 2,
        scratch_shapes=[
            packed,
            pltpu.VMEM(wig.shape, BF16),
            atoms,
            pltpu.VMEM((flat, LANES), F32),
            ghost,
            ghost,
            pltpu.VMEM((8 * LANES, LANES), F32),
            atoms,
            atoms,
            atoms,
            pltpu.SemaphoreType.DMA((6,)),
            pltpu.SemaphoreType.DMA((3,)),
        ],
        compiler_params=pltpu.CompilerParams(vmem_limit_bytes=60 * 1024 * 1024),
    )(message, wig, node_rows, own_grad, below_grad, above_grad, send, dst, env)

    def restore(x):
        return jnp.transpose(x.reshape(NODE, 32, LANES), (2, 0, 1))

    return restore(updated), restore(node_grad)


def solution(mesh):
    in_specs = (
        P("space", None, "morder"),
        P("space"),
        P("space"),
        P("space"),
        P("space", None, None),
        P("space"),
        P(),
        P(),
        P(),
        P(),
        P(),
        P("space", None, "morder"),
    )
    out_specs = (P("space", None, "morder"), P("space", None, "morder"))
    return jax.shard_map(shards, mesh=mesh, in_specs=in_specs, out_specs=out_specs, check_vma=False)
```
